32 devices in a mesh: grp: 2 (over y), gy: 8 (over z, x), gx: 2 (over core).
Axes of the slice: x: 2, y: 2, z: 4, core: 2. Of those that a mesh axis runs over, the one named last changes fastest.
Arguments:
- context: bfloat16 [64, 512, 384], P(('grp', 'gy'), 'gx'), parts along dimension 0, may hold values from -6 to 6
- kernels: bfloat16 [3, 3456, 384], replicated, may hold values from -0.109375 to 0.109375
- final_kernel: bfloat16 [3456, 384], replicated, may hold values from -0.109375 to 0.109375
Outputs:
- forecast: bfloat16 [64, 512, 384], P('grp', ('gy', 'gx')), parts along dimension 0
The draws below stay inside these ranges and needn't reach their ends.
There are 2 independent parts, one for each index of `grp`. The reference program is written for one: setup_inputs(seed, part) draws one part's arguments, and reference() takes and returns one part's arrays. A program takes and returns all parts, laid end to end along the dimension named above; an argument that names none is the same for every part. Nothing has to cross between parts.
All inputs are finite; a program needn't handle non-finite values.
Results may differ from the reference program's by a relative error of at most 0.014.
Values may be sent and summed in bfloat16 or wider, within the bound.
No kernel may reach another device: no remote copies, remote signals or barrier semaphores. Data moves between devices by JAX's collectives and lax.ppermute only.
A program may use at most 64 MiB of HBM per device.

```python
import jax
import jax.numpy as jnp

C = 384
LAYERS = 3
NY = 32
NX = 512


def level_of(rng, shape, split, smallest, largest):
    gain = 1.0
    for axis_at, blocks in split:
        draws = jax.random.uniform(jax.random.fold_in(jax.random.fold_in(rng, 6), axis_at), (blocks,), jnp.float32, smallest / len(split), largest / len(split))
        gain = gain * jnp.repeat(jnp.exp(draws), shape[axis_at] // blocks).reshape((-1,) + (1,) * (len(shape) - 1 - axis_at))
    return gain


def bell_draw(own_key, shape, deviation, limit, shards=(), dtype=jnp.bfloat16):
    values = jax.random.normal(own_key, shape, jnp.float32) * deviation
    if len(shards) > 0:
        values = level_of(own_key, shape, shards, -0.22, 0.18) * values
    return jnp.clip(values, min=-limit, max=limit).astype(dtype)


def setup_inputs(seed: int = 0, part: int = 0) -> dict:
    keys = jax.random.split(jax.random.key(seed), 4)
    part_keys = jax.random.split(jax.random.fold_in(keys[3], part), 4)
    return {
        "context": bell_draw(part_keys[0], (NY, NX, C), 1.0, 6.0, ((0, 8), (1, 2))),
        "kernels": bell_draw(keys[1], (LAYERS, 9 * C, C), (9 * C) ** -0.5, 0.109375),
        "final_kernel": bell_draw(keys[2], (9 * C, C), (9 * C) ** -0.5, 0.109375),
    }


dilation_list = (1, 8, 16)


def activate(stream):
    return jax.nn.gelu(stream.astype(jnp.float32)).astype(jnp.bfloat16)


def dilated_conv(activated, kernel, dilation):
    extent_rows, extent_cols, channels = activated.shape
    padded = jnp.pad(activated, ((dilation, dilation), (dilation, dilation), (0, 0)))
    summed = jnp.zeros((extent_rows * extent_cols, channels), jnp.float32)
    for row_tap in range(3):
        for col_tap in range(3):
            window = padded[row_tap * dilation:row_tap * dilation + extent_rows, col_tap * dilation:col_tap * dilation + extent_cols]
            tap_index = 3 * row_tap + col_tap
            kernel_block = kernel[tap_index * channels:(tap_index + 1) * channels]
            summed = summed + jnp.dot(window.reshape(extent_rows * extent_cols, channels), kernel_block, preferred_element_type=jnp.float32)
    return summed.reshape(extent_rows, extent_cols, channels)


def widen_cols(extended):
    values = extended.astype(jnp.float32)
    inner_count = values.shape[1] - 2
    middle = values[:, 1:inner_count + 1]
    even_cols = 0.25 * values[:, 0:inner_count] + 0.75 * middle
    odd_cols = 0.75 * middle + 0.25 * values[:, 2:inner_count + 2]
    return jnp.stack([even_cols, odd_cols], axis=2).reshape(values.shape[0], 2 * inner_count, values.shape[2])


def widen_rows(values):
    above = jnp.concatenate([values[:1], values[:-1]], axis=0)
    below = jnp.concatenate([values[1:], values[-1:]], axis=0)
    even_rows = 0.25 * above + 0.75 * values
    odd_rows = 0.75 * values + 0.25 * below
    return jnp.stack([even_rows, odd_rows], axis=1).reshape(2 * values.shape[0], values.shape[1], values.shape[2])


def reference(context, kernels, final_kernel):
    stream = context
    for layer_index, dilation in enumerate(dilation_list):
        branch = dilated_conv(activate(stream), kernels[layer_index], dilation)
        stream = (stream.astype(jnp.float32) + branch).astype(jnp.bfloat16)
    rows_total = stream.shape[0]
    cols_total = stream.shape[1]
    cropped = stream[rows_total // 4:3 * rows_total // 4, cols_total // 4:3 * cols_total // 4]
    extended = jnp.concatenate([cropped[:, :1], cropped, cropped[:, -1:]], axis=1)
    upsampled = widen_rows(widen_cols(extended)).astype(jnp.bfloat16)
    return dilated_conv(upsampled, final_kernel, 1).astype(jnp.bfloat16)
```

```python
import functools

import jax
import jax.numpy as jnp
from jax import lax
from jax.experimental import pallas as pl
from jax.experimental.pallas import tpu as pltpu
from jax.sharding import PartitionSpec as P

dilation_list = (1, 8, 16)
F32 = jnp.float32
BF16 = jnp.bfloat16


def padded_2(cells, sides, width):
    for axis, dim in sides:
        count = lax.axis_size(axis)
        ends = count - 1
        head = lax.slice_in_dim(cells, 0, width, axis=dim)
        tail = lax.slice_in_dim(cells, cells.shape[dim] - width, cells.shape[dim], axis=dim)
        cells = jnp.concatenate(
            [
                lax.ppermute(tail, axis, [(i, (i + 1) % count) for i in range(ends)]),
                cells,
                lax.ppermute(head, axis, [((i + 1) % count, i) for i in range(ends)]),
            ],
            axis=dim,
        )
    return cells


def shifted(value, axis, by):
    size = lax.axis_size(axis)
    pairs = [(i, i + by) for i in range(size) if 0 <= i + by < size]
    return lax.ppermute(value, axis, pairs)


def activate(stream):
    return jax.nn.gelu(stream.astype(F32)).astype(BF16)


def conv_taps(row_bands, center, dilation, out_cols, kernel):
    pieces = []
    for row_band in row_bands:
        for col_tap in range(3):
            offset = center + (col_tap - 1) * dilation
            pieces.append(row_band[:, offset : offset + out_cols])
    stacked = jnp.concatenate(pieces, axis=-1)
    result = jnp.dot(
        stacked.reshape(-1, stacked.shape[-1]), kernel, preferred_element_type=F32
    )
    return result.reshape(stacked.shape[0], out_cols, kernel.shape[1])


def tile_layer(stream, kernel, dilation):
    activated = activate(stream)
    rows_here = stream.shape[0]
    if dilation == 1:
        rimmed = padded_2(activated, (("gy", 0), ("gx", 1)), 1)
        row_bands = [rimmed[0:rows_here], rimmed[1 : rows_here + 1], rimmed[2 : rows_here + 2]]
    else:
        widened = padded_2(activated, (("gx", 1),), dilation)
        hop_count = dilation // rows_here
        upper_rows = shifted(widened, "gy", hop_count)
        lower_rows = shifted(widened, "gy", -hop_count)
        row_bands = [upper_rows, widened, lower_rows]
    branch = conv_taps(row_bands, dilation, dilation, stream.shape[1], kernel)
    return (stream.astype(F32) + branch).astype(BF16)


def recut_crop(stream):
    rows_here, cols_here, channels = stream.shape
    count_gy = lax.axis_size("gy")
    count_gx = lax.axis_size("gx")
    targets = count_gy * count_gx
    grid_cols = cols_here * count_gx
    strip_cols = grid_cols // 2 // targets
    blocks = stream.reshape(rows_here, cols_here // strip_cols, strip_cols, channels)
    spare = jnp.zeros((rows_here, targets, strip_cols, channels), BF16)
    padded = jnp.concatenate([spare, blocks, spare], axis=1)
    offset = (
        targets + grid_cols // 4 // strip_cols - lax.axis_index("gx") * (cols_here // strip_cols)
    )
    outgoing = lax.dynamic_slice_in_dim(padded, offset, targets, 1)
    target = lax.axis_index(("gy", "gx"))
    owner = (grid_cols // 4 + target * strip_cols) // cols_here
    arrived = lax.all_to_all(outgoing, ("gy", "gx"), split_axis=1, concat_axis=0, tiled=True)
    arrived = arrived.reshape(count_gy, count_gx, rows_here, strip_cols, channels)
    chosen = lax.dynamic_index_in_dim(arrived, owner, 1, keepdims=False)
    grid_rows = count_gy * rows_here
    whole_rows = chosen.reshape(grid_rows, strip_cols, channels)
    return whole_rows[grid_rows // 4 : 3 * grid_rows // 4]


def widen_cols(extended):
    values = extended.astype(F32)
    inner_count = values.shape[1] - 2
    middle = values[:, 1 : inner_count + 1]
    even_cols = 0.25 * values[:, 0:inner_count] + 0.75 * middle
    odd_cols = 0.75 * middle + 0.25 * values[:, 2 : inner_count + 2]
    return jnp.stack([even_cols, odd_cols], axis=2).reshape(
        values.shape[0], 2 * inner_count, values.shape[2]
    )


def widen_rows(values):
    above = jnp.concatenate([values[:1], values[:-1]], axis=0)
    below = jnp.concatenate([values[1:], values[-1:]], axis=0)
    even_rows = 0.25 * above + 0.75 * values
    odd_rows = 0.75 * values + 0.25 * below
    return jnp.stack([even_rows, odd_rows], axis=1).reshape(
        2 * values.shape[0], values.shape[1], values.shape[2]
    )


def general_shards(context, kernels, final_kernel):
    stream = context
    for layer_index, dilation in enumerate(dilation_list):
        stream = tile_layer(stream, kernels[layer_index], dilation)
    cropped = recut_crop(stream)
    target = lax.axis_index(("gy", "gx"))
    last_target = lax.axis_size(("gy", "gx")) - 1
    rimmed = padded_2(cropped, ((("gy", "gx"), 1),), 1)
    first_col = jnp.where(target == 0, rimmed[:, 1:2], rimmed[:, 0:1])
    final_col = jnp.where(target == last_target, rimmed[:, -2:-1], rimmed[:, -1:])
    rimmed = jnp.concatenate([first_col, rimmed[:, 1:-1], final_col], axis=1)
    upsampled = widen_rows(widen_cols(rimmed)).astype(BF16)
    up_rimmed = padded_2(upsampled, ((("gy", "gx"), 1),), 1)
    up_rows = up_rimmed.shape[0]
    padded = jnp.pad(up_rimmed, ((1, 1), (0, 0), (0, 0)))
    row_bands = [padded[0:up_rows], padded[1 : up_rows + 1], padded[2 : up_rows + 2]]
    result = conv_taps(row_bands, 1, 1, up_rimmed.shape[1] - 2, final_kernel)
    return result.astype(BF16)


C = 384
OWN = 160
BAND = 320
BAND_AT = 96
WIN = 184
MID = 168
CUT = 136
PART = 40
VMEM_LIMIT = 56 * 1024 * 1024

INNER_STEPS = (((0, 3), (3, 1)), ((1, 3), (2, 1)), ((0, 1), (2, 3)))


def gelu(values):
    return jax.nn.gelu(values.astype(F32))


def dot(left, right):
    return jnp.dot(left, right, preferred_element_type=F32)


def place():
    gy = lax.axis_index("gy")
    return gy // 2, gy % 2, lax.axis_index("gx")


def load_taps(weights_ref, layer, taps_ref, sems):
    copies = []
    for tap in range(3):
        rows = pl.ds(tap * 3 * C, 3 * C)
        source = weights_ref.at[rows] if layer is None else weights_ref.at[layer, rows]
        copies.append(pltpu.make_async_copy(source, taps_ref.at[rows], sems.at[tap]))
    for copy in copies:
        copy.start()
    return copies


def row_taps(taps_ref, tap):
    return taps_ref[tap * 3 * C : (tap + 1) * 3 * C, :]


def lay_band(values, lanes_ref):
    act = gelu(values)
    lanes_ref[:, C : 2 * C] = act.astype(BF16)
    lanes_ref[:, 0:C] = pltpu.roll(act, 1, 0).astype(BF16)
    lanes_ref[:, 2 * C : 3 * C] = pltpu.roll(act, BAND - 1, 0).astype(BF16)


def send_windows(stream_ref, z, steps, flip, send_refs, own_ref):
    def window(half):
        start = pl.multiple_of(8 + 120 * half, 8)
        return stream_ref[pl.ds(start, WIN), :].astype(BF16)

    for step, send_ref in zip(steps, send_refs):
        half = sum(jnp.where(z == (source ^ flip), (target ^ flip) // 2, 0) for source, target in step)
        send_ref[...] = window(half)
    own_ref[...] = window(z // 2)


def inner_kernel(own_ref, got_ref, weights_ref, s1, s2, s3, keep, taps_ref, sems, band_ref, lanes_ref, stream_ref):
    copies = load_taps(weights_ref, 0, taps_ref, sems)
    z, _, c = place()
    own_at = pl.multiple_of(c * OWN, OWN)
    got_at = pl.multiple_of((1 - c) * OWN, OWN)
    for row in range(3):
        band_ref[row, pl.ds(own_at, OWN), :] = own_ref[row]
        band_ref[row, pl.ds(got_at, OWN), :] = got_ref[row]
    total = band_ref[1].astype(F32)
    for row in range(3):
        lay_band(band_ref[row], lanes_ref.at[row])
    for row in range(3):
        copies[row].wait()
        total = total + dot(lanes_ref[row], row_taps(taps_ref, row))
    stream_ref[...] = total
    send_windows(stream_ref, z, INNER_STEPS, 0, (s1, s2, s3), keep)


def outer_kernel(own_ref, got_ref, halo_ref, weights_ref, s1, s2, s3, keep, taps_ref, sems, band_ref, lanes_ref, stream_ref):
    copies = load_taps(weights_ref, 0, taps_ref, sems)
    z, _, c = place()
    own_at = pl.multiple_of(c * OWN, OWN)
    got_at = pl.multiple_of((1 - c) * OWN, OWN)
    for slot in range(2):
        row = slot + c
        band_ref[row, pl.ds(own_at, OWN), :] = own_ref[row]
        band_ref[row, pl.ds(got_at, OWN), :] = got_ref[row]
    centre = band_ref[2 * c]
    lay_band(centre, lanes_ref.at[1])
    lay_band(band_ref[1], lanes_ref.at[2 - 2 * c])
    lay_band(halo_ref[0], lanes_ref.at[2 * c])
    total = centre.astype(F32)
    for row in range(3):
        copies[row].wait()
        total = total + dot(lanes_ref[row], row_taps(taps_ref, row))
    stream_ref[...] = total
    send_windows(stream_ref, z, INNER_STEPS, 1, (s1, s2, s3), keep)


def middle_kernel(ik, i1, i2, i3, ok, o1, o2, o3, weights_ref, parts_ref, taps2_ref, sems2, taps3_ref, sems3, rows_ref, lanes_ref, mid_ref, lanes3_ref, cut_ref):
    copies2 = load_taps(weights_ref, 1, taps2_ref, sems2)
    copies3 = load_taps(weights_ref, 2, taps3_ref, sems3)
    z, _, _ = place()
    half = z // 2

    def source_of(steps, flip, at):
        return sum(jnp.where(z == (target ^ flip), source ^ flip, 0) for source, target in steps[at])

    def take(refs, flip):
        rows_ref[z] = refs[0][...]
        for at in range(3):
            rows_ref[source_of(INNER_STEPS, flip, at)] = refs[at + 1][...]

    @pl.when(z % 2 == 1)
    def _():
        take((ik, i1, i2, i3), 0)

    @pl.when(z % 2 == 0)
    def _():
        take((ok, o1, o2, o3), 1)

    for row in range(4):
        act = gelu(rows_ref[row])
        for tap in range(3):
            lanes_ref[row, :, tap * C : (tap + 1) * C] = act[8 * tap : 8 * tap + MID].astype(BF16)
        mid_ref[row] = rows_ref[row].astype(F32)[8 : 8 + MID]
    flat = lambda first, count: lanes_ref[first : first + count].reshape(count * MID, 3 * C)
    for tap, first_in, first_out, count in ((0, 0, 1, 3), (1, 0, 0, 4), (2, 1, 0, 3)):
        copies2[tap].wait()
        product = dot(flat(first_in, count), row_taps(taps2_ref, tap)).reshape(count, MID, C)
        mid_ref[first_out : first_out + count] += product
    for row in range(4):
        rounded = mid_ref[row].astype(BF16)
        act = gelu(rounded)
        for tap in range(3):
            lanes3_ref[row, :, tap * C : (tap + 1) * C] = act[16 * tap : 16 * tap + CUT].astype(BF16)
        if row in (1, 2):
            cut_ref[row - 1] = rounded.astype(F32)[16 : 16 + CUT]
    for copy in copies3:
        copy.wait()
    cut_ref[0] += dot(lanes3_ref[1], row_taps(taps3_ref, 1)) + dot(lanes3_ref[3], row_taps(taps3_ref, 2))
    cut_ref[1] += dot(lanes3_ref[2], row_taps(taps3_ref, 1)) + dot(lanes3_ref[0], row_taps(taps3_ref, 0))
    for target in range(8):
        base = pl.multiple_of(8 * half + 16 * target, 8)
        left = jnp.maximum(base - 1, 0)
        right = jnp.minimum(base + 16, CUT - 1)
        for row in range(2):
            parts_ref[target, 16 * row : 16 * row + 16, :] = cut_ref[row, pl.ds(base, 16), :].astype(BF16)
        edges = [cut_ref[row, pl.ds(at, 1), :] for row in range(2) for at in (left, right)]
        parts_ref[target, 32:40, :] = jnp.concatenate(edges + edges, axis=0).astype(BF16)


def final_kernel_body(parts_ref, weights_ref, out_ref, taps_ref, sems, ext_ref, planes_ref, lanes_ref, total_ref):
    copies = load_taps(weights_ref, None, taps_ref, sems)
    z, x, c = place()
    target = 4 * z + 2 * x + c
    keep_first = jnp.where(target == 0, 0.0, 1.0)
    keep_last = jnp.where(target == 15, 0.0, 1.0)
    for source in range(8):
        inner, sx, sc = source // 4, (source // 2) % 2, source % 2
        rho = 4 * sx + ((0, 3), (1, 2))[inner][sc]
        edges = parts_ref[source, 32:40, :].astype(F32)
        for row in range(2):
            ext_ref[rho + 8 * row, 8:24, :] = parts_ref[source, 16 * row : 16 * row + 16, :].astype(F32)
            ext_ref[rho + 8 * row, 7:8, :] = edges[2 * row : 2 * row + 1]
            ext_ref[rho + 8 * row, 24:25, :] = edges[2 * row + 1 : 2 * row + 2]
    column = lax.broadcasted_iota(jnp.int32, (16, C), 0)
    first_mask = jnp.where(column == 0, keep_first, 1.0)
    last_mask = jnp.where(column == 15, keep_last, 1.0)
    for row in range(16):
        now = ext_ref[row, 8:24, :]
        before = ext_ref[row, 7:23, :]
        after = ext_ref[row, 9:25, :]
        planes_ref[row, 0] = (0.75 * before + 0.25 * now) * first_mask
        planes_ref[row, 1] = 0.25 * before + 0.75 * now
        planes_ref[row, 2] = 0.75 * now + 0.25 * after
        planes_ref[row, 3] = (0.25 * now + 0.75 * after) * last_mask
    zeros = jnp.zeros((16, 4 * C), BF16)
    lanes_ref[0:16, :] = zeros
    lanes_ref[33 * 16 : 34 * 16, :] = zeros
    for row in range(16):
        above, below = max(row - 1, 0), min(row + 1, 15)
        for plane in range(4):
            value = planes_ref[row, plane]
            at = slice(plane * C, (plane + 1) * C)
            first = 16 * (1 + 2 * row)
            lanes_ref[first : first + 16, at] = (0.25 * planes_ref[above, plane] + 0.75 * value).astype(BF16)
            lanes_ref[first + 16 : first + 32, at] = (0.75 * value + 0.25 * planes_ref[below, plane]).astype(BF16)
    for copy in copies:
        copy.wait()
    for parity in range(2):
        total = jnp.zeros((512, C), F32)
        for tap in range(3):
            total = total + dot(
                lanes_ref[16 * tap : 16 * tap + 512, parity * C : (parity + 3) * C], row_taps(taps_ref, tap)
            )
        for lane in range(3):
            total_ref[lane, pl.ds(parity, 512, stride=2), :] = total[:, 128 * lane : 128 * lane + 128]
    for lane in range(3):
        out_ref[:, :, 128 * lane : 128 * lane + 128] = total_ref[lane].reshape(32, 32, 128).astype(BF16)


VM = pl.BlockSpec(memory_space=pltpu.VMEM)
ANY = pl.BlockSpec(memory_space=pl.ANY)


def local_call(body, operands, weights, out_shapes, scratch, flops):
    moved = sum(o.size * 2 for o in operands) + sum(2 * functools.reduce(lambda a, b: a * b, s) for s in out_shapes)
    return pl.pallas_call(
        body,
        out_shape=tuple(jax.ShapeDtypeStruct(s, BF16) for s in out_shapes),
        in_specs=[VM] * len(operands) + [ANY],
        out_specs=tuple(VM for _ in out_shapes),
        scratch_shapes=scratch,
        compiler_params=pltpu.CompilerParams(vmem_limit_bytes=VMEM_LIMIT),
        cost_estimate=pl.CostEstimate(flops=flops, bytes_accessed=moved + 9 * C * C * 2, transcendentals=0),
    )(*operands, weights)


TAPS = [pltpu.VMEM((9 * C, C), BF16), pltpu.SemaphoreType.DMA((3,))]


def residue_shards(context, kernels, final_kernel):
    c = lax.axis_index("gx")
    col_at = BAND_AT * (1 - c)
    own = lax.dynamic_slice(context, (c, col_at, 0), (3, OWN, C))
    send = lax.dynamic_slice(context, (1 - c, col_at, 0), (3, OWN, C))
    got = lax.ppermute(send, "gx", [(0, 1), (1, 0)])
    mine = jnp.where(c == 0, own[0:1], own[2:3])
    theirs = jnp.where(c == 0, got[0:1], got[2:3])
    rim = jnp.where(
        c == 0, jnp.concatenate([mine, theirs], axis=1), jnp.concatenate([theirs, mine], axis=1)
    )
    places = lax.axis_size("gy") * 2
    pairs = []
    for left in range(1, places - 1, 2):
        pairs += [(left, left + 1), (left + 1, left)]
    halo = lax.ppermute(rim, ("gy", "gx"), pairs)

    window = (WIN, C)
    row_scratch = TAPS + [
        pltpu.VMEM((3, BAND, C), BF16),
        pltpu.VMEM((3, BAND, 3 * C), BF16),
        pltpu.VMEM((BAND, C), F32),
    ]
    row_flops = 2 * BAND * 9 * C * C
    inner = local_call(inner_kernel, (own, got), kernels, [window] * 4, row_scratch, row_flops)
    outer = local_call(outer_kernel, (own, got, halo), kernels, [window] * 4, row_scratch, row_flops)

    def along_z(value, step, flip):
        pairs = [(4 * (s ^ flip) + i, 4 * (t ^ flip) + i) for s, t in step for i in range(4)]
        return lax.ppermute(value, ("gy", "gx"), pairs)

    inner_in = [along_z(v, s, 0) for v, s in zip(inner[:3], INNER_STEPS)]
    outer_in = [along_z(v, s, 1) for v, s in zip(outer[:3], INNER_STEPS)]
    middle_scratch = TAPS + TAPS + [
        pltpu.VMEM((4, WIN, C), BF16),
        pltpu.VMEM((4, MID, 3 * C), BF16),
        pltpu.VMEM((4, MID, C), F32),
        pltpu.VMEM((4, CUT, 3 * C), BF16),
        pltpu.VMEM((2, CUT, C), F32),
    ]
    (parts,) = local_call(
        middle_kernel,
        (inner[3], *inner_in, outer[3], *outer_in),
        kernels,
        [(8, PART, C)],
        middle_scratch,
        2 * (10 * MID + 4 * CUT) * 3 * C * C,
    )
    groups = [[8 * half + i for i in range(8)] for half in range(places // 8)]
    parts = lax.all_to_all(parts, ("gy", "gx"), 0, 0, axis_index_groups=groups, tiled=True)
    final_scratch = TAPS + [
        pltpu.VMEM((16, 32, C), F32),
        pltpu.VMEM((16, 4, 16, C), F32),
        pltpu.VMEM((34 * 16, 4 * C), BF16),
        pltpu.VMEM((3, 1024, 128), F32),
    ]
    (out,) = local_call(
        final_kernel_body, (parts,), final_kernel, [(32, 32, C)], final_scratch, 2 * 1024 * 9 * C * C
    )
    return out


def solution(mesh):
    placed = (P(("grp", "gy"), "gx", None), P(), P())
    body = residue_shards if (mesh.shape["gy"], mesh.shape["gx"]) == (8, 2) else general_shards
    return jax.shard_map(
        body, mesh=mesh, in_specs=placed, out_specs=P("grp", ("gy", "gx"), None), check_vma=False
    )
```

```python
import functools

import jax
import jax.numpy as jnp
from jax import lax
from jax.experimental import pallas as pl
from jax.experimental.pallas import tpu as pltpu
from jax.sharding import PartitionSpec as P

dilation_list = (1, 8, 16)
F32 = jnp.float32
BF16 = jnp.bfloat16


def padded_2(cells, sides, width):
    for axis, dim in sides:
        count = lax.axis_size(axis)
        ends = count - 1
        head = lax.slice_in_dim(cells, 0, width, axis=dim)
        tail = lax.slice_in_dim(cells, cells.shape[dim] - width, cells.shape[dim], axis=dim)
        cells = jnp.concatenate(
            [
                lax.ppermute(tail, axis, [(i, (i + 1) % count) for i in range(ends)]),
                cells,
                lax.ppermute(head, axis, [((i + 1) % count, i) for i in range(ends)]),
            ],
            axis=dim,
        )
    return cells


def shifted(value, axis, by):
    size = lax.axis_size(axis)
    pairs = [(i, i + by) for i in range(size) if 0 <= i + by < size]
    return lax.ppermute(value, axis, pairs)


def activate(stream):
    return jax.nn.gelu(stream.astype(F32)).astype(BF16)


def conv_taps(row_bands, center, dilation, out_cols, kernel):
    pieces = []
    for row_band in row_bands:
        for col_tap in range(3):
            offset = center + (col_tap - 1) * dilation
            pieces.append(row_band[:, offset : offset + out_cols])
    stacked = jnp.concatenate(pieces, axis=-1)
    result = jnp.dot(
        stacked.reshape(-1, stacked.shape[-1]), kernel, preferred_element_type=F32
    )
    return result.reshape(stacked.shape[0], out_cols, kernel.shape[1])


def tile_layer(stream, kernel, dilation):
    activated = activate(stream)
    rows_here = stream.shape[0]
    if dilation == 1:
        rimmed = padded_2(activated, (("gy", 0), ("gx", 1)), 1)
        row_bands = [rimmed[0:rows_here], rimmed[1 : rows_here + 1], rimmed[2 : rows_here + 2]]
    else:
        widened = padded_2(activated, (("gx", 1),), dilation)
        hop_count = dilation // rows_here
        upper_rows = shifted(widened, "gy", hop_count)
        lower_rows = shifted(widened, "gy", -hop_count)
        row_bands = [upper_rows, widened, lower_rows]
    branch = conv_taps(row_bands, dilation, dilation, stream.shape[1], kernel)
    return (stream.astype(F32) + branch).astype(BF16)


def recut_crop(stream):
    rows_here, cols_here, channels = stream.shape
    count_gy = lax.axis_size("gy")
    count_gx = lax.axis_size("gx")
    targets = count_gy * count_gx
    grid_cols = cols_here * count_gx
    strip_cols = grid_cols // 2 // targets
    blocks = stream.reshape(rows_here, cols_here // strip_cols, strip_cols, channels)
    spare = jnp.zeros((rows_here, targets, strip_cols, channels), BF16)
    padded = jnp.concatenate([spare, blocks, spare], axis=1)
    offset = (
        targets + grid_cols // 4 // strip_cols - lax.axis_index("gx") * (cols_here // strip_cols)
    )
    outgoing = lax.dynamic_slice_in_dim(padded, offset, targets, 1)
    target = lax.axis_index(("gy", "gx"))
    owner = (grid_cols // 4 + target * strip_cols) // cols_here
    arrived = lax.all_to_all(outgoing, ("gy", "gx"), split_axis=1, concat_axis=0, tiled=True)
    arrived = arrived.reshape(count_gy, count_gx, rows_here, strip_cols, channels)
    chosen = lax.dynamic_index_in_dim(arrived, owner, 1, keepdims=False)
    grid_rows = count_gy * rows_here
    whole_rows = chosen.reshape(grid_rows, strip_cols, channels)
    return whole_rows[grid_rows // 4 : 3 * grid_rows // 4]


def widen_cols(extended):
    values = extended.astype(F32)
    inner_count = values.shape[1] - 2
    middle = values[:, 1 : inner_count + 1]
    even_cols = 0.25 * values[:, 0:inner_count] + 0.75 * middle
    odd_cols = 0.75 * middle + 0.25 * values[:, 2 : inner_count + 2]
    return jnp.stack([even_cols, odd_cols], axis=2).reshape(
        values.shape[0], 2 * inner_count, values.shape[2]
    )


def widen_rows(values):
    above = jnp.concatenate([values[:1], values[:-1]], axis=0)
    below = jnp.concatenate([values[1:], values[-1:]], axis=0)
    even_rows = 0.25 * above + 0.75 * values
    odd_rows = 0.75 * values + 0.25 * below
    return jnp.stack([even_rows, odd_rows], axis=1).reshape(
        2 * values.shape[0], values.shape[1], values.shape[2]
    )


def general_shards(context, kernels, final_kernel):
    stream = context
    for layer_index, dilation in enumerate(dilation_list):
        stream = tile_layer(stream, kernels[layer_index], dilation)
    cropped = recut_crop(stream)
    target = lax.axis_index(("gy", "gx"))
    last_target = lax.axis_size(("gy", "gx")) - 1
    rimmed = padded_2(cropped, ((("gy", "gx"), 1),), 1)
    first_col = jnp.where(target == 0, rimmed[:, 1:2], rimmed[:, 0:1])
    final_col = jnp.where(target == last_target, rimmed[:, -2:-1], rimmed[:, -1:])
    rimmed = jnp.concatenate([first_col, rimmed[:, 1:-1], final_col], axis=1)
    upsampled = widen_rows(widen_cols(rimmed)).astype(BF16)
    up_rimmed = padded_2(upsampled, ((("gy", "gx"), 1),), 1)
    up_rows = up_rimmed.shape[0]
    padded = jnp.pad(up_rimmed, ((1, 1), (0, 0), (0, 0)))
    row_bands = [padded[0:up_rows], padded[1 : up_rows + 1], padded[2 : up_rows + 2]]
    result = conv_taps(row_bands, 1, 1, up_rimmed.shape[1] - 2, final_kernel)
    return result.astype(BF16)


C = 384
OWN = 160
BAND = 320
BAND_AT = 96
WIN = 184
MID = 168
CUT = 136
PART = 40
VMEM_LIMIT = 32 * 1024 * 1024


def gelu(values):
    return jax.nn.gelu(values.astype(F32))


def dot(left, right):
    return jnp.dot(left, right, preferred_element_type=F32)


def place():
    gy = lax.axis_index("gy")
    return gy // 2, gy % 2, lax.axis_index("gx")


def row_taps(taps_ref, tap):
    return taps_ref[tap * 3 * C : (tap + 1) * 3 * C, :]


def lay_band(values, lanes_ref):
    act = gelu(values)
    lanes_ref[:, C : 2 * C] = act.astype(BF16)
    lanes_ref[:, 0:C] = pltpu.roll(act, 1, 0).astype(BF16)
    lanes_ref[:, 2 * C : 3 * C] = pltpu.roll(act, BAND - 1, 0).astype(BF16)


def window(stream_ref, half):
    start = pl.multiple_of(8 + 120 * half, 8)
    return stream_ref[pl.ds(start, WIN), :].astype(BF16)


def edge_kernel(context_ref, top_ref, low_ref, sems):
    _, _, c = place()
    at = pl.multiple_of(BAND_AT * (1 - c), 32)
    copies = [
        pltpu.make_async_copy(context_ref.at[row, pl.ds(at, OWN)], edge_ref, sems.at[slot])
        for slot, (row, edge_ref) in enumerate(((3 * c, top_ref), (3 - 3 * c, low_ref)))
    ]
    for copy in copies:
        copy.start()
    for copy in copies:
        copy.wait()


def inner_kernel(context_ref, kernels_ref, got_ref, inner_ref, part_ref, taps_ref, next_ref, sems, own_ref, band_ref, lanes_ref):
    _, _, c = place()
    at = pl.multiple_of(BAND_AT * (1 - c), 32)
    own = pltpu.make_async_copy(context_ref.at[pl.ds(c, 3), pl.ds(at, OWN)], own_ref, sems.at[0])
    taps = pltpu.make_async_copy(kernels_ref.at[0], taps_ref, sems.at[1])
    later = pltpu.make_async_copy(kernels_ref.at[pl.ds(1, 2)], next_ref, sems.at[2])
    for copy in (own, taps, later):
        copy.start()
    own.wait()
    got_at = pl.multiple_of(BAND_AT * c, 32)
    for row in range(3):
        band_ref[row, pl.ds(pl.multiple_of((1 - c) * OWN, OWN), OWN), :] = got_ref[row + c, pl.ds(got_at, OWN), :]
        band_ref[row, pl.ds(pl.multiple_of(c * OWN, OWN), OWN), :] = own_ref[row]
    for row in range(3):
        lay_band(band_ref[row], lanes_ref.at[row])
    taps.wait()
    inner_ref[...] = (
        band_ref[1].astype(F32)
        + dot(lanes_ref[0], row_taps(taps_ref, 0))
        + dot(lanes_ref[1], row_taps(taps_ref, 1))
        + dot(lanes_ref[2], row_taps(taps_ref, 2))
    )

    @pl.when(c == 0)
    def _():
        part_ref[...] = (
            band_ref[0].astype(F32)
            + dot(lanes_ref[0], row_taps(taps_ref, 1))
            + dot(lanes_ref[1], row_taps(taps_ref, 2))
        )

    @pl.when(c == 1)
    def _():
        part_ref[...] = (
            band_ref[2].astype(F32)
            + dot(lanes_ref[1], row_taps(taps_ref, 0))
            + dot(lanes_ref[2], row_taps(taps_ref, 1))
        )

    later.wait()


def outer_kernel(side_ref, cross_ref, inner_ref, part_ref, taps_ref, s1, s2, s3, keep, halo_ref, lanes_ref, outer_ref):
    z, x, c = place()
    inside = jnp.where(jnp.logical_or(4 * z + 2 * x + c == 0, 4 * z + 2 * x + c == 15), 0.0, 1.0)
    halo_ref[pl.ds(pl.multiple_of(c * OWN, OWN), OWN), :] = side_ref[...]
    halo_ref[pl.ds(pl.multiple_of((1 - c) * OWN, OWN), OWN), :] = cross_ref[...]
    lay_band(halo_ref[...].astype(F32) * inside, lanes_ref)
    start = pl.multiple_of(6 * C * c, 6 * C)
    outer_ref[...] = part_ref[...] + dot(lanes_ref[...], taps_ref[pl.ds(start, 3 * C), :])
    near, far = z // 2, 1 - z // 2

    @pl.when(z % 2 == 0)
    def _():
        keep[...] = window(outer_ref, near)
        s2[...] = window(outer_ref, far)
        s1[...] = window(inner_ref, near)
        s3[...] = window(inner_ref, far)

    @pl.when(z % 2 == 1)
    def _():
        keep[...] = window(inner_ref, near)
        s2[...] = window(inner_ref, far)
        s1[...] = window(outer_ref, near)
        s3[...] = window(outer_ref, far)


def middle_kernel(keep, r1, r2, r3, taps_ref, parts_ref, rows_ref, lanes_ref, mid_ref, lanes3_ref, cut_ref):
    z, _, _ = place()
    half = z // 2
    zx = lambda k: z + k - 2 * sum(((z // b) % 2) * b for b in (1, 2) if k & b)
    rows_ref[z] = keep[...]
    rows_ref[zx(1)] = r1[...]
    rows_ref[zx(3)] = r3[...]
    rows_ref[zx(2)] = r2[...]
    for row in range(4):
        act = gelu(rows_ref[row])
        for tap in range(3):
            lanes_ref[row, :, tap * C : (tap + 1) * C] = act[8 * tap : 8 * tap + MID].astype(BF16)
        mid_ref[row] = rows_ref[row].astype(F32)[8 : 8 + MID]
    flat = lambda first, count: lanes_ref[first : first + count].reshape(count * MID, 3 * C)
    for tap, first_in, first_out, count in ((0, 0, 1, 3), (1, 0, 0, 4), (2, 1, 0, 3)):
        product = dot(flat(first_in, count), row_taps(taps_ref.at[0], tap)).reshape(count, MID, C)
        mid_ref[first_out : first_out + count] += product
    for row in range(4):
        rounded = mid_ref[row].astype(BF16)
        act = gelu(rounded)
        for tap in range(3):
            lanes3_ref[row, :, tap * C : (tap + 1) * C] = act[16 * tap : 16 * tap + CUT].astype(BF16)
        if row in (1, 2):
            cut_ref[row - 1] = rounded.astype(F32)[16 : 16 + CUT]
    cut_ref[0] += dot(lanes3_ref[1], row_taps(taps_ref.at[1], 1)) + dot(lanes3_ref[3], row_taps(taps_ref.at[1], 2))
    cut_ref[1] += dot(lanes3_ref[2], row_taps(taps_ref.at[1], 1)) + dot(lanes3_ref[0], row_taps(taps_ref.at[1], 0))
    for target in range(8):
        base = pl.multiple_of(8 * half + 16 * target, 8)
        left = jnp.maximum(base - 1, 0)
        right = jnp.minimum(base + 16, CUT - 1)
        for row in range(2):
            parts_ref[target, 16 * row : 16 * row + 16, :] = cut_ref[row, pl.ds(base, 16), :].astype(BF16)
        edges = [cut_ref[row, pl.ds(at, 1), :] for row in range(2) for at in (left, right)]
        parts_ref[target, 32:40, :] = jnp.concatenate(edges + edges, axis=0).astype(BF16)


def final_kernel_body(parts_ref, taps_ref, out_ref, ext_ref, planes_ref, lanes_ref, total_ref):
    z, x, c = place()
    target = 4 * z + 2 * x + c
    keep_first = jnp.where(target == 0, 0.0, 1.0)
    keep_last = jnp.where(target == 15, 0.0, 1.0)
    for source in range(8):
        inner, sx, sc = source // 4, (source // 2) % 2, source % 2
        rho = 4 * sx + ((0, 3), (1, 2))[inner][sc]
        edges = parts_ref[source, 32:40, :].astype(F32)
        for row in range(2):
            ext_ref[rho + 8 * row, 8:24, :] = parts_ref[source, 16 * row : 16 * row + 16, :].astype(F32)
            ext_ref[rho + 8 * row, 7:8, :] = edges[2 * row : 2 * row + 1]
            ext_ref[rho + 8 * row, 24:25, :] = edges[2 * row + 1 : 2 * row + 2]
    column = lax.broadcasted_iota(jnp.int32, (16, C), 0)
    first_mask = jnp.where(column == 0, keep_first, 1.0)
    last_mask = jnp.where(column == 15, keep_last, 1.0)
    for row in range(16):
        now = ext_ref[row, 8:24, :]
        before = ext_ref[row, 7:23, :]
        after = ext_ref[row, 9:25, :]
        planes_ref[row, 0] = (0.75 * before + 0.25 * now) * first_mask
        planes_ref[row, 1] = 0.25 * before + 0.75 * now
        planes_ref[row, 2] = 0.75 * now + 0.25 * after
        planes_ref[row, 3] = (0.25 * now + 0.75 * after) * last_mask
    zeros = jnp.zeros((16, 4 * C), BF16)
    lanes_ref[0:16, :] = zeros
    lanes_ref[33 * 16 : 34 * 16, :] = zeros
    for row in range(16):
        above, below = max(row - 1, 0), min(row + 1, 15)
        for plane in range(4):
            value = planes_ref[row, plane]
            at = slice(plane * C, (plane + 1) * C)
            first = 16 * (1 + 2 * row)
            lanes_ref[first : first + 16, at] = (0.25 * planes_ref[above, plane] + 0.75 * value).astype(BF16)
            lanes_ref[first + 16 : first + 32, at] = (0.75 * value + 0.25 * planes_ref[below, plane]).astype(BF16)
    for parity in range(2):
        total = jnp.zeros((512, C), F32)
        for tap in range(3):
            total = total + dot(
                lanes_ref[16 * tap : 16 * tap + 512, parity * C : (parity + 3) * C], row_taps(taps_ref, tap)
            )
        for lane in range(3):
            total_ref[lane, pl.ds(parity, 512, stride=2), :] = total[:, 128 * lane : 128 * lane + 128]
    for lane in range(3):
        out_ref[:, :, 128 * lane : 128 * lane + 128] = total_ref[lane].reshape(32, 32, 128).astype(BF16)


VM = pl.BlockSpec(memory_space=pltpu.VMEM)
HBM = pl.BlockSpec(memory_space=pltpu.HBM)


def in_vmem(value):
    return pltpu.with_memory_space_constraint(value, pltpu.VMEM)


def local_call(body, operands, outs, scratch, flops, hbm_operands=(), hbm_out=False):
    shape = (lambda s, d: jax.ShapeDtypeStruct(s, d)) if hbm_out else pltpu.VMEM
    return pl.pallas_call(
        body,
        out_shape=tuple(shape(s, d) for s, d in outs),
        in_specs=[HBM] * len(hbm_operands) + [VM] * len(operands),
        out_specs=tuple(VM for _ in outs),
        scratch_shapes=scratch,
        compiler_params=pltpu.CompilerParams(vmem_limit_bytes=VMEM_LIMIT),
        cost_estimate=pl.CostEstimate(flops=flops, bytes_accessed=0, transcendentals=0),
    )(
        *[pltpu.with_memory_space_constraint(value, pltpu.HBM) for value in hbm_operands],
        *[in_vmem(value) for value in operands],
    )


def residue_shards(context, kernels, final_kernel):
    got = lax.ppermute(context, "gx", [(0, 1), (1, 0)])
    edge = ((OWN, C), BF16)
    cross, side = local_call(
        edge_kernel, (), [edge, edge], [pltpu.SemaphoreType.DMA((2,))], 0, hbm_operands=(context,)
    )
    chips = lax.axis_size("gy")
    places = 2 * chips
    pairs = [(0, 0), (places - 1, places - 1)]
    for left in range(1, places - 1, 2):
        pairs += [(left, left + 1), (left + 1, left)]
    cross = lax.ppermute(cross, ("gy", "gx"), pairs)
    pairs = [(places - 2, places - 1), (1, 0)]
    for chip in range(chips - 1):
        pairs += [(2 * chip, 2 * chip + 2), (2 * chip + 3, 2 * chip + 1)]
    side = lax.ppermute(side, ("gy", "gx"), pairs)

    row_flops = 2 * BAND * 3 * C * C
    win = ((WIN, C), BF16)
    row = ((BAND, C), F32)
    inner, part, taps, next_taps = local_call(
        inner_kernel,
        (got,),
        [row, row, ((9 * C, C), BF16), ((2, 9 * C, C), BF16)],
        [
            pltpu.SemaphoreType.DMA((3,)),
            pltpu.VMEM((3, OWN, C), BF16),
            pltpu.VMEM((3, BAND, C), BF16),
            pltpu.VMEM((3, BAND, 3 * C), BF16),
        ],
        5 * row_flops,
        hbm_operands=(context, kernels),
    )

    def along_z(value, step):
        pairs = [(4 * s + i, 4 * (s ^ step) + i) for s in range(4) for i in range(4)]
        return lax.ppermute(value, ("gy", "gx"), pairs)

    s1, s2, s3, keep = local_call(
        outer_kernel,
        (side, cross, inner, part, taps),
        [win] * 4,
        [pltpu.VMEM((BAND, C), BF16), pltpu.VMEM((BAND, 3 * C), BF16), pltpu.VMEM((BAND, C), F32)],
        row_flops,
    )
    r3 = along_z(s3, 3)
    r2 = along_z(s2, 2)
    r1 = along_z(s1, 1)
    (parts,) = local_call(
        middle_kernel,
        (keep, r1, r2, r3, next_taps),
        [((8, PART, C), BF16)],
        [
            pltpu.VMEM((4, WIN, C), BF16),
            pltpu.VMEM((4, MID, 3 * C), BF16),
            pltpu.VMEM((4, MID, C), F32),
            pltpu.VMEM((4, CUT, 3 * C), BF16),
            pltpu.VMEM((2, CUT, C), F32),
        ],
        2 * (10 * MID + 4 * CUT) * 3 * C * C,
    )
    groups = [[8 * half + i for i in range(8)] for half in range(places // 8)]
    parts = lax.all_to_all(parts, ("gy", "gx"), 0, 0, axis_index_groups=groups, tiled=True)
    (out,) = local_call(
        final_kernel_body,
        (parts, final_kernel),
        [((32, 32, C), BF16)],
        [
            pltpu.VMEM((16, 32, C), F32),
            pltpu.VMEM((16, 4, 16, C), F32),
            pltpu.VMEM((34 * 16, 4 * C), BF16),
            pltpu.VMEM((3, 1024, 128), F32),
        ],
        2 * 1024 * 9 * C * C,
        hbm_out=True,
    )
    return out


def solution(mesh):
    placed = (P(("grp", "gy"), "gx", None), P(), P())
    body = residue_shards if (mesh.shape["gy"], mesh.shape["gx"]) == (8, 2) else general_shards
    return jax.shard_map(
        body, mesh=mesh, in_specs=placed, out_specs=P("grp", ("gy", "gx"), None), check_vma=False
    )
```

```python
import functools

import jax
import jax.numpy as jnp
from jax import lax
from jax.experimental import pallas as pl
from jax.experimental.pallas import tpu as pltpu
from jax.sharding import PartitionSpec as P

dilation_list = (1, 8, 16)
F32 = jnp.float32
BF16 = jnp.bfloat16


def padded_2(cells, sides, width):
    for axis, dim in sides:
        count = lax.axis_size(axis)
        ends = count - 1
        head = lax.slice_in_dim(cells, 0, width, axis=dim)
        tail = lax.slice_in_dim(cells, cells.shape[dim] - width, cells.shape[dim], axis=dim)
        cells = jnp.concatenate(
            [
                lax.ppermute(tail, axis, [(i, (i + 1) % count) for i in range(ends)]),
                cells,
                lax.ppermute(head, axis, [((i + 1) % count, i) for i in range(ends)]),
            ],
            axis=dim,
        )
    return cells


def shifted(value, axis, by):
    size = lax.axis_size(axis)
    pairs = [(i, i + by) for i in range(size) if 0 <= i + by < size]
    return lax.ppermute(value, axis, pairs)


def activate(stream):
    return jax.nn.gelu(stream.astype(F32)).astype(BF16)


def conv_taps(row_bands, center, dilation, out_cols, kernel):
    pieces = []
    for row_band in row_bands:
        for col_tap in range(3):
            offset = center + (col_tap - 1) * dilation
            pieces.append(row_band[:, offset : offset + out_cols])
    stacked = jnp.concatenate(pieces, axis=-1)
    result = jnp.dot(
        stacked.reshape(-1, stacked.shape[-1]), kernel, preferred_element_type=F32
    )
    return result.reshape(stacked.shape[0], out_cols, kernel.shape[1])


def tile_layer(stream, kernel, dilation):
    activated = activate(stream)
    rows_here = stream.shape[0]
    if dilation == 1:
        rimmed = padded_2(activated, (("gy", 0), ("gx", 1)), 1)
        row_bands = [rimmed[0:rows_here], rimmed[1 : rows_here + 1], rimmed[2 : rows_here + 2]]
    else:
        widened = padded_2(activated, (("gx", 1),), dilation)
        hop_count = dilation // rows_here
        upper_rows = shifted(widened, "gy", hop_count)
        lower_rows = shifted(widened, "gy", -hop_count)
        row_bands = [upper_rows, widened, lower_rows]
    branch = conv_taps(row_bands, dilation, dilation, stream.shape[1], kernel)
    return (stream.astype(F32) + branch).astype(BF16)


def recut_crop(stream):
    rows_here, cols_here, channels = stream.shape
    count_gy = lax.axis_size("gy")
    count_gx = lax.axis_size("gx")
    targets = count_gy * count_gx
    grid_cols = cols_here * count_gx
    strip_cols = grid_cols // 2 // targets
    blocks = stream.reshape(rows_here, cols_here // strip_cols, strip_cols, channels)
    spare = jnp.zeros((rows_here, targets, strip_cols, channels), BF16)
    padded = jnp.concatenate([spare, blocks, spare], axis=1)
    offset = (
        targets + grid_cols // 4 // strip_cols - lax.axis_index("gx") * (cols_here // strip_cols)
    )
    outgoing = lax.dynamic_slice_in_dim(padded, offset, targets, 1)
    target = lax.axis_index(("gy", "gx"))
    owner = (grid_cols // 4 + target * strip_cols) // cols_here
    arrived = lax.all_to_all(outgoing, ("gy", "gx"), split_axis=1, concat_axis=0, tiled=True)
    arrived = arrived.reshape(count_gy, count_gx, rows_here, strip_cols, channels)
    chosen = lax.dynamic_index_in_dim(arrived, owner, 1, keepdims=False)
    grid_rows = count_gy * rows_here
    whole_rows = chosen.reshape(grid_rows, strip_cols, channels)
    return whole_rows[grid_rows // 4 : 3 * grid_rows // 4]


def widen_cols(extended):
    values = extended.astype(F32)
    inner_count = values.shape[1] - 2
    middle = values[:, 1 : inner_count + 1]
    even_cols = 0.25 * values[:, 0:inner_count] + 0.75 * middle
    odd_cols = 0.75 * middle + 0.25 * values[:, 2 : inner_count + 2]
    return jnp.stack([even_cols, odd_cols], axis=2).reshape(
        values.shape[0], 2 * inner_count, values.shape[2]
    )


def widen_rows(values):
    above = jnp.concatenate([values[:1], values[:-1]], axis=0)
    below = jnp.concatenate([values[1:], values[-1:]], axis=0)
    even_rows = 0.25 * above + 0.75 * values
    odd_rows = 0.75 * values + 0.25 * below
    return jnp.stack([even_rows, odd_rows], axis=1).reshape(
        2 * values.shape[0], values.shape[1], values.shape[2]
    )


def general_shards(context, kernels, final_kernel):
    stream = context
    for layer_index, dilation in enumerate(dilation_list):
        stream = tile_layer(stream, kernels[layer_index], dilation)
    cropped = recut_crop(stream)
    target = lax.axis_index(("gy", "gx"))
    last_target = lax.axis_size(("gy", "gx")) - 1
    rimmed = padded_2(cropped, ((("gy", "gx"), 1),), 1)
    first_col = jnp.where(target == 0, rimmed[:, 1:2], rimmed[:, 0:1])
    final_col = jnp.where(target == last_target, rimmed[:, -2:-1], rimmed[:, -1:])
    rimmed = jnp.concatenate([first_col, rimmed[:, 1:-1], final_col], axis=1)
    upsampled = widen_rows(widen_cols(rimmed)).astype(BF16)
    up_rimmed = padded_2(upsampled, ((("gy", "gx"), 1),), 1)
    up_rows = up_rimmed.shape[0]
    padded = jnp.pad(up_rimmed, ((1, 1), (0, 0), (0, 0)))
    row_bands = [padded[0:up_rows], padded[1 : up_rows + 1], padded[2 : up_rows + 2]]
    result = conv_taps(row_bands, 1, 1, up_rimmed.shape[1] - 2, final_kernel)
    return result.astype(BF16)


C = 384
OWN = 160
BAND = 320
BAND_AT = 96
WIN = 184
MID = 168
CUT = 136
PART = 40
VMEM_LIMIT = 32 * 1024 * 1024
STEPS = (3, 1, 2)


def gelu(values):
    return jax.nn.gelu(values.astype(F32))


def dot(left, right):
    return jnp.dot(left, right, preferred_element_type=F32)


def place():
    gy = lax.axis_index("gy")
    return gy // 2, gy % 2, lax.axis_index("gx")


def row_taps(taps_ref, tap):
    return taps_ref[tap * 3 * C : (tap + 1) * 3 * C, :]


def lay_band(values, lanes_ref):
    act = gelu(values)
    lanes_ref[:, C : 2 * C] = act.astype(BF16)
    lanes_ref[:, 0:C] = pltpu.roll(act, 1, 0).astype(BF16)
    lanes_ref[:, 2 * C : 3 * C] = pltpu.roll(act, BAND - 1, 0).astype(BF16)


def window(stream_ref, half):
    start = pl.multiple_of(8 + 120 * half, 8)
    return stream_ref[pl.ds(start, WIN), :].astype(BF16)


def edge_kernel(context_ref, top_ref, low_ref, sems):
    _, _, c = place()
    at = pl.multiple_of(BAND_AT * (1 - c), 32)
    copies = [
        pltpu.make_async_copy(context_ref.at[row, pl.ds(at, OWN)], edge_ref, sems.at[slot])
        for slot, (row, edge_ref) in enumerate(((3 * c, top_ref), (3 - 3 * c, low_ref)))
    ]
    for copy in copies:
        copy.start()
    for copy in copies:
        copy.wait()


def inner_kernel(context_ref, kernels_ref, got_ref, inner_ref, part_ref, taps_ref, next_ref, sems, own_ref, band_ref, lanes_ref):
    _, _, c = place()
    at = pl.multiple_of(BAND_AT * (1 - c), 32)
    own = pltpu.make_async_copy(context_ref.at[pl.ds(c, 3), pl.ds(at, OWN)], own_ref, sems.at[0])
    taps = pltpu.make_async_copy(kernels_ref.at[0], taps_ref, sems.at[1])
    later = pltpu.make_async_copy(kernels_ref.at[pl.ds(1, 2)], next_ref, sems.at[2])
    for copy in (own, taps, later):
        copy.start()
    own.wait()
    got_at = pl.multiple_of(BAND_AT * c, 32)
    for row in range(3):
        band_ref[row, pl.ds(pl.multiple_of((1 - c) * OWN, OWN), OWN), :] = got_ref[row + c, pl.ds(got_at, OWN), :]
        band_ref[row, pl.ds(pl.multiple_of(c * OWN, OWN), OWN), :] = own_ref[row]
    for row in range(3):
        lay_band(band_ref[row], lanes_ref.at[row])
    taps.wait()
    inner_ref[...] = (
        band_ref[1].astype(F32)
        + dot(lanes_ref[0], row_taps(taps_ref, 0))
        + dot(lanes_ref[1], row_taps(taps_ref, 1))
        + dot(lanes_ref[2], row_taps(taps_ref, 2))
    )

    @pl.when(c == 0)
    def _():
        part_ref[...] = (
            band_ref[0].astype(F32)
            + dot(lanes_ref[0], row_taps(taps_ref, 1))
            + dot(lanes_ref[1], row_taps(taps_ref, 2))
        )

    @pl.when(c == 1)
    def _():
        part_ref[...] = (
            band_ref[2].astype(F32)
            + dot(lanes_ref[1], row_taps(taps_ref, 0))
            + dot(lanes_ref[2], row_taps(taps_ref, 1))
        )

    later.wait()


def outer_kernel(side_ref, cross_ref, inner_ref, part_ref, taps_ref, s1, s2, s3, keep, halo_ref, lanes_ref, outer_ref):
    z, x, c = place()
    inside = jnp.where(jnp.logical_or(4 * z + 2 * x + c == 0, 4 * z + 2 * x + c == 15), 0.0, 1.0)
    halo_ref[pl.ds(pl.multiple_of(c * OWN, OWN), OWN), :] = side_ref[...]
    halo_ref[pl.ds(pl.multiple_of((1 - c) * OWN, OWN), OWN), :] = cross_ref[...]
    lay_band(halo_ref[...].astype(F32) * inside, lanes_ref)
    start = pl.multiple_of(6 * C * c, 6 * C)
    outer_ref[...] = part_ref[...] + dot(lanes_ref[...], taps_ref[pl.ds(start, 3 * C), :])
    near, far = z // 2, 1 - z // 2

    @pl.when(z % 2 == 0)
    def _():
        keep[...] = window(outer_ref, near)
        s2[...] = window(outer_ref, far)
        s1[...] = window(inner_ref, near)
        s3[...] = window(inner_ref, far)

    @pl.when(z % 2 == 1)
    def _():
        keep[...] = window(inner_ref, near)
        s2[...] = window(inner_ref, far)
        s1[...] = window(outer_ref, near)
        s3[...] = window(outer_ref, far)


def exchanged(z, step):
    low, high = z % 2, z // 2
    return (low + (step % 2) * (1 - 2 * low)) + 2 * (high + (step // 2) * (1 - 2 * high))


def add_row(step, row_ref, taps_ref, sum_ref, lanes_ref):
    z, _, _ = place()
    row = exchanged(z, step)
    act = gelu(row_ref[...])
    for tap in range(3):
        lanes_ref[:, tap * C : (tap + 1) * C] = act[8 * tap : 8 * tap + MID].astype(BF16)
    sum_ref[row + 1] += row_ref[...].astype(F32)[8 : 8 + MID]
    for tap in range(3):
        sum_ref[row + 2 - tap] += dot(lanes_ref[...], row_taps(taps_ref.at[0], tap))


def first_kernel(row_ref, taps_ref, sum_ref, lanes_ref):
    sum_ref[...] = jnp.zeros_like(sum_ref)
    add_row(0, row_ref, taps_ref, sum_ref, lanes_ref)


def next_kernel(step, row_ref, taps_ref, before_ref, sum_ref, lanes_ref):
    add_row(step, row_ref, taps_ref, sum_ref, lanes_ref)


def last_kernel(step, row_ref, taps_ref, before_ref, sum_ref, parts_ref, lanes_ref, lanes3_ref, cut_ref):
    add_row(step, row_ref, taps_ref, sum_ref, lanes_ref)
    z, _, _ = place()
    half = z // 2
    for row in range(4):
        rounded = sum_ref[row + 1].astype(BF16)
        act = gelu(rounded)
        for tap in range(3):
            lanes3_ref[row, :, tap * C : (tap + 1) * C] = act[16 * tap : 16 * tap + CUT].astype(BF16)
        if row in (1, 2):
            cut_ref[row - 1] = rounded.astype(F32)[16 : 16 + CUT]
    cut_ref[0] += dot(lanes3_ref[1], row_taps(taps_ref.at[1], 1)) + dot(lanes3_ref[3], row_taps(taps_ref.at[1], 2))
    cut_ref[1] += dot(lanes3_ref[2], row_taps(taps_ref.at[1], 1)) + dot(lanes3_ref[0], row_taps(taps_ref.at[1], 0))
    for target in range(8):
        base = pl.multiple_of(8 * half + 16 * target, 8)
        left = jnp.maximum(base - 1, 0)
        right = jnp.minimum(base + 16, CUT - 1)
        for row in range(2):
            parts_ref[target, 16 * row : 16 * row + 16, :] = cut_ref[row, pl.ds(base, 16), :].astype(BF16)
        edges = [cut_ref[row, pl.ds(at, 1), :] for row in range(2) for at in (left, right)]
        parts_ref[target, 32:40, :] = jnp.concatenate(edges + edges, axis=0).astype(BF16)


def final_kernel_body(parts_ref, taps_ref, out_ref, ext_ref, planes_ref, lanes_ref, total_ref):
    z, x, c = place()
    target = 4 * z + 2 * x + c
    keep_first = jnp.where(target == 0, 0.0, 1.0)
    keep_last = jnp.where(target == 15, 0.0, 1.0)
    for source in range(8):
        inner, sx, sc = source // 4, (source // 2) % 2, source % 2
        rho = 4 * sx + ((0, 3), (1, 2))[inner][sc]
        edges = parts_ref[source, 32:40, :].astype(F32)
        for row in range(2):
            ext_ref[rho + 8 * row, 8:24, :] = parts_ref[source, 16 * row : 16 * row + 16, :].astype(F32)
            ext_ref[rho + 8 * row, 7:8, :] = edges[2 * row : 2 * row + 1]
            ext_ref[rho + 8 * row, 24:25, :] = edges[2 * row + 1 : 2 * row + 2]
    column = lax.broadcasted_iota(jnp.int32, (16, C), 0)
    first_mask = jnp.where(column == 0, keep_first, 1.0)
    last_mask = jnp.where(column == 15, keep_last, 1.0)
    for row in range(16):
        now = ext_ref[row, 8:24, :]
        before = ext_ref[row, 7:23, :]
        after = ext_ref[row, 9:25, :]
        planes_ref[row, 0] = (0.75 * before + 0.25 * now) * first_mask
        planes_ref[row, 1] = 0.25 * before + 0.75 * now
        planes_ref[row, 2] = 0.75 * now + 0.25 * after
        planes_ref[row, 3] = (0.25 * now + 0.75 * after) * last_mask
    zeros = jnp.zeros((16, 4 * C), BF16)
    lanes_ref[0:16, :] = zeros
    lanes_ref[33 * 16 : 34 * 16, :] = zeros
    for row in range(16):
        above, below = max(row - 1, 0), min(row + 1, 15)
        for plane in range(4):
            value = planes_ref[row, plane]
            at = slice(plane * C, (plane + 1) * C)
            first = 16 * (1 + 2 * row)
            lanes_ref[first : first + 16, at] = (0.25 * planes_ref[above, plane] + 0.75 * value).astype(BF16)
            lanes_ref[first + 16 : first + 32, at] = (0.75 * value + 0.25 * planes_ref[below, plane]).astype(BF16)
    for parity in range(2):
        total = jnp.zeros((512, C), F32)
        for tap in range(3):
            total = total + dot(
                lanes_ref[16 * tap : 16 * tap + 512, parity * C : (parity + 3) * C], row_taps(taps_ref, tap)
            )
        for lane in range(3):
            total_ref[lane, pl.ds(parity, 512, stride=2), :] = total[:, 128 * lane : 128 * lane + 128]
    for lane in range(3):
        out_ref[:, :, 128 * lane : 128 * lane + 128] = total_ref[lane].reshape(32, 32, 128).astype(BF16)


VM = pl.BlockSpec(memory_space=pltpu.VMEM)
HBM = pl.BlockSpec(memory_space=pltpu.HBM)


def in_vmem(value):
    return pltpu.with_memory_space_constraint(value, pltpu.VMEM)


def local_call(body, operands, outs, scratch, flops, hbm_operands=(), hbm_out=False, aliases={}):
    shape = (lambda s, d: jax.ShapeDtypeStruct(s, d)) if hbm_out else pltpu.VMEM
    return pl.pallas_call(
        body,
        out_shape=tuple(shape(s, d) for s, d in outs),
        in_specs=[HBM] * len(hbm_operands) + [VM] * len(operands),
        out_specs=tuple(VM for _ in outs),
        scratch_shapes=scratch,
        input_output_aliases=aliases,
        compiler_params=pltpu.CompilerParams(vmem_limit_bytes=VMEM_LIMIT),
        cost_estimate=pl.CostEstimate(flops=flops, bytes_accessed=0, transcendentals=0),
    )(
        *[pltpu.with_memory_space_constraint(value, pltpu.HBM) for value in hbm_operands],
        *[in_vmem(value) for value in operands],
    )


def residue_shards(context, kernels, final_kernel):
    got = lax.ppermute(context, "gx", [(0, 1), (1, 0)])
    edge = ((OWN, C), BF16)
    cross, side = local_call(
        edge_kernel, (), [edge, edge], [pltpu.SemaphoreType.DMA((2,))], 0, hbm_operands=(context,)
    )
    chips = lax.axis_size("gy")
    places = 2 * chips
    pairs = [(0, 0), (places - 1, places - 1)]
    for left in range(1, places - 1, 2):
        pairs += [(left, left + 1), (left + 1, left)]
    cross = lax.ppermute(cross, ("gy", "gx"), pairs)
    pairs = [(places - 2, places - 1), (1, 0)]
    for chip in range(chips - 1):
        pairs += [(2 * chip, 2 * chip + 2), (2 * chip + 3, 2 * chip + 1)]
    side = lax.ppermute(side, ("gy", "gx"), pairs)

    row_flops = 2 * BAND * 3 * C * C
    win = ((WIN, C), BF16)
    row = ((BAND, C), F32)
    inner, part, taps, next_taps = local_call(
        inner_kernel,
        (got,),
        [row, row, ((9 * C, C), BF16), ((2, 9 * C, C), BF16)],
        [
            pltpu.SemaphoreType.DMA((3,)),
            pltpu.VMEM((3, OWN, C), BF16),
            pltpu.VMEM((3, BAND, C), BF16),
            pltpu.VMEM((3, BAND, 3 * C), BF16),
        ],
        5 * row_flops,
        hbm_operands=(context, kernels),
    )

    def along_z(value, step):
        pairs = [(4 * s + i, 4 * (s ^ step) + i) for s in range(4) for i in range(4)]
        return lax.ppermute(value, ("gy", "gx"), pairs)

    s1, s2, s3, keep = local_call(
        outer_kernel,
        (side, cross, inner, part, taps),
        [win] * 4,
        [pltpu.VMEM((BAND, C), BF16), pltpu.VMEM((BAND, 3 * C), BF16), pltpu.VMEM((BAND, C), F32)],
        row_flops,
    )
    sent = {3: s3, 2: s2, 1: s1}
    came = {step: along_z(sent[step], step) for step in STEPS}
    sums = ((6, MID, C), F32)
    lanes = pltpu.VMEM((MID, 3 * C), BF16)
    term_flops = 2 * MID * 9 * C * C
    (total,) = local_call(first_kernel, (keep, next_taps), [sums], [lanes], term_flops)
    for step in STEPS[:2]:
        (total,) = local_call(
            functools.partial(next_kernel, step),
            (came[step], next_taps, total),
            [sums],
            [lanes],
            term_flops,
            aliases={2: 0},
        )
    _, parts = local_call(
        functools.partial(last_kernel, STEPS[2]),
        (came[STEPS[2]], next_taps, total),
        [sums, ((8, PART, C), BF16)],
        [lanes, pltpu.VMEM((4, CUT, 3 * C), BF16), pltpu.VMEM((2, CUT, C), F32)],
        2 * term_flops,
        aliases={2: 0},
    )
    groups = [[8 * half + i for i in range(8)] for half in range(places // 8)]
    parts = lax.all_to_all(parts, ("gy", "gx"), 0, 0, axis_index_groups=groups, tiled=True)
    (out,) = local_call(
        final_kernel_body,
        (parts, final_kernel),
        [((32, 32, C), BF16)],
        [
            pltpu.VMEM((16, 32, C), F32),
            pltpu.VMEM((16, 4, 16, C), F32),
            pltpu.VMEM((34 * 16, 4 * C), BF16),
            pltpu.VMEM((3, 1024, 128), F32),
        ],
        2 * 1024 * 9 * C * C,
        hbm_out=True,
    )
    return out


def solution(mesh):
    placed = (P(("grp", "gy"), "gx", None), P(), P())
    body = residue_shards if (mesh.shape["gy"], mesh.shape["gx"]) == (8, 2) else general_shards
    return jax.shard_map(
        body, mesh=mesh, in_specs=placed, out_specs=P("grp", ("gy", "gx"), None), check_vma=False
    )
```

```python
import functools

import jax
import jax.numpy as jnp
from jax import lax
from jax.experimental import pallas as pl
from jax.experimental.pallas import tpu as pltpu
from jax.sharding import PartitionSpec as P

dilation_list = (1, 8, 16)
F32 = jnp.float32
BF16 = jnp.bfloat16


def padded_2(cells, sides, width):
    for axis, dim in sides:
        count = lax.axis_size(axis)
        ends = count - 1
        head = lax.slice_in_dim(cells, 0, width, axis=dim)
        tail = lax.slice_in_dim(cells, cells.shape[dim] - width, cells.shape[dim], axis=dim)
        cells = jnp.concatenate(
            [
                lax.ppermute(tail, axis, [(i, (i + 1) % count) for i in range(ends)]),
                cells,
                lax.ppermute(head, axis, [((i + 1) % count, i) for i in range(ends)]),
            ],
            axis=dim,
        )
    return cells


def shifted(value, axis, by):
    size = lax.axis_size(axis)
    pairs = [(i, i + by) for i in range(size) if 0 <= i + by < size]
    return lax.ppermute(value, axis, pairs)


def activate(stream):
    return jax.nn.gelu(stream.astype(F32)).astype(BF16)


def conv_taps(row_bands, center, dilation, out_cols, kernel):
    pieces = []
    for row_band in row_bands:
        for col_tap in range(3):
            offset = center + (col_tap - 1) * dilation
            pieces.append(row_band[:, offset : offset + out_cols])
    stacked = jnp.concatenate(pieces, axis=-1)
    result = jnp.dot(
        stacked.reshape(-1, stacked.shape[-1]), kernel, preferred_element_type=F32
    )
    return result.reshape(stacked.shape[0], out_cols, kernel.shape[1])


def tile_layer(stream, kernel, dilation):
    activated = activate(stream)
    rows_here = stream.shape[0]
    if dilation == 1:
        rimmed = padded_2(activated, (("gy", 0), ("gx", 1)), 1)
        row_bands = [rimmed[0:rows_here], rimmed[1 : rows_here + 1], rimmed[2 : rows_here + 2]]
    else:
        widened = padded_2(activated, (("gx", 1),), dilation)
        hop_count = dilation // rows_here
        upper_rows = shifted(widened, "gy", hop_count)
        lower_rows = shifted(widened, "gy", -hop_count)
        row_bands = [upper_rows, widened, lower_rows]
    branch = conv_taps(row_bands, dilation, dilation, stream.shape[1], kernel)
    return (stream.astype(F32) + branch).astype(BF16)


def recut_crop(stream):
    rows_here, cols_here, channels = stream.shape
    count_gy = lax.axis_size("gy")
    count_gx = lax.axis_size("gx")
    targets = count_gy * count_gx
    grid_cols = cols_here * count_gx
    strip_cols = grid_cols // 2 // targets
    blocks = stream.reshape(rows_here, cols_here // strip_cols, strip_cols, channels)
    spare = jnp.zeros((rows_here, targets, strip_cols, channels), BF16)
    padded = jnp.concatenate([spare, blocks, spare], axis=1)
    offset = (
        targets + grid_cols // 4 // strip_cols - lax.axis_index("gx") * (cols_here // strip_cols)
    )
    outgoing = lax.dynamic_slice_in_dim(padded, offset, targets, 1)
    target = lax.axis_index(("gy", "gx"))
    owner = (grid_cols // 4 + target * strip_cols) // cols_here
    arrived = lax.all_to_all(outgoing, ("gy", "gx"), split_axis=1, concat_axis=0, tiled=True)
    arrived = arrived.reshape(count_gy, count_gx, rows_here, strip_cols, channels)
    chosen = lax.dynamic_index_in_dim(arrived, owner, 1, keepdims=False)
    grid_rows = count_gy * rows_here
    whole_rows = chosen.reshape(grid_rows, strip_cols, channels)
    return whole_rows[grid_rows // 4 : 3 * grid_rows // 4]


def widen_cols(extended):
    values = extended.astype(F32)
    inner_count = values.shape[1] - 2
    middle = values[:, 1 : inner_count + 1]
    even_cols = 0.25 * values[:, 0:inner_count] + 0.75 * middle
    odd_cols = 0.75 * middle + 0.25 * values[:, 2 : inner_count + 2]
    return jnp.stack([even_cols, odd_cols], axis=2).reshape(
        values.shape[0], 2 * inner_count, values.shape[2]
    )


def widen_rows(values):
    above = jnp.concatenate([values[:1], values[:-1]], axis=0)
    below = jnp.concatenate([values[1:], values[-1:]], axis=0)
    even_rows = 0.25 * above + 0.75 * values
    odd_rows = 0.75 * values + 0.25 * below
    return jnp.stack([even_rows, odd_rows], axis=1).reshape(
        2 * values.shape[0], values.shape[1], values.shape[2]
    )


def general_shards(context, kernels, final_kernel):
    stream = context
    for layer_index, dilation in enumerate(dilation_list):
        stream = tile_layer(stream, kernels[layer_index], dilation)
    cropped = recut_crop(stream)
    target = lax.axis_index(("gy", "gx"))
    last_target = lax.axis_size(("gy", "gx")) - 1
    rimmed = padded_2(cropped, ((("gy", "gx"), 1),), 1)
    first_col = jnp.where(target == 0, rimmed[:, 1:2], rimmed[:, 0:1])
    final_col = jnp.where(target == last_target, rimmed[:, -2:-1], rimmed[:, -1:])
    rimmed = jnp.concatenate([first_col, rimmed[:, 1:-1], final_col], axis=1)
    upsampled = widen_rows(widen_cols(rimmed)).astype(BF16)
    up_rimmed = padded_2(upsampled, ((("gy", "gx"), 1),), 1)
    up_rows = up_rimmed.shape[0]
    padded = jnp.pad(up_rimmed, ((1, 1), (0, 0), (0, 0)))
    row_bands = [padded[0:up_rows], padded[1 : up_rows + 1], padded[2 : up_rows + 2]]
    result = conv_taps(row_bands, 1, 1, up_rimmed.shape[1] - 2, final_kernel)
    return result.astype(BF16)


C = 384
OWN = 160
BAND = 320
BAND_AT = 96
WIN = 184
MID = 168
CUT = 136
PART = 40
VMEM_LIMIT = 32 * 1024 * 1024
CHUNK = 16
STEPS = (3, 1, 2)


def gelu(values):
    return jax.nn.gelu(values.astype(F32))


def dot(left, right):
    return jnp.dot(left, right, preferred_element_type=F32)


def place():
    gy = lax.axis_index("gy")
    return gy // 2, gy % 2, lax.axis_index("gx")


def row_taps(taps_ref, tap):
    return taps_ref[tap * 3 * C : (tap + 1) * 3 * C, :]


def lay_band(values, lanes_ref):
    act = gelu(values)
    lanes_ref[:, C : 2 * C] = act.astype(BF16)
    lanes_ref[:, 0:C] = pltpu.roll(act, 1, 0).astype(BF16)
    lanes_ref[:, 2 * C : 3 * C] = pltpu.roll(act, BAND - 1, 0).astype(BF16)


def window(stream_ref, half):
    start = pl.multiple_of(8 + 120 * half, 8)
    return stream_ref[pl.ds(start, WIN), :].astype(BF16)


def edge_kernel(context_ref, top_ref, low_ref, sems):
    _, _, c = place()
    at = pl.multiple_of(BAND_AT * (1 - c), 32)
    copies = [
        pltpu.make_async_copy(context_ref.at[row, pl.ds(at, OWN)], edge_ref, sems.at[slot])
        for slot, (row, edge_ref) in enumerate(((3 * c, top_ref), (3 - 3 * c, low_ref)))
    ]
    for copy in copies:
        copy.start()
    for copy in copies:
        copy.wait()


def inner_kernel(context_ref, kernels_ref, got_ref, inner_ref, part_ref, taps_ref, next_ref, sems, own_ref, band_ref, lanes_ref):
    _, _, c = place()
    at = pl.multiple_of(BAND_AT * (1 - c), 32)
    own = pltpu.make_async_copy(context_ref.at[pl.ds(c, 3), pl.ds(at, OWN)], own_ref, sems.at[0])
    taps = pltpu.make_async_copy(kernels_ref.at[0], taps_ref, sems.at[1])
    later = pltpu.make_async_copy(kernels_ref.at[pl.ds(1, 2)], next_ref, sems.at[2])
    for copy in (own, taps, later):
        copy.start()
    own.wait()
    got_at = pl.multiple_of(BAND_AT * c, 32)
    for row in range(3):
        band_ref[row, pl.ds(pl.multiple_of((1 - c) * OWN, OWN), OWN), :] = got_ref[row + c, pl.ds(got_at, OWN), :]
        band_ref[row, pl.ds(pl.multiple_of(c * OWN, OWN), OWN), :] = own_ref[row]
    for row in range(3):
        lay_band(band_ref[row], lanes_ref.at[row])
    taps.wait()
    inner_ref[...] = (
        band_ref[1].astype(F32)
        + dot(lanes_ref[0], row_taps(taps_ref, 0))
        + dot(lanes_ref[1], row_taps(taps_ref, 1))
        + dot(lanes_ref[2], row_taps(taps_ref, 2))
    )

    @pl.when(c == 0)
    def _():
        part_ref[...] = (
            band_ref[0].astype(F32)
            + dot(lanes_ref[0], row_taps(taps_ref, 1))
            + dot(lanes_ref[1], row_taps(taps_ref, 2))
        )

    @pl.when(c == 1)
    def _():
        part_ref[...] = (
            band_ref[2].astype(F32)
            + dot(lanes_ref[1], row_taps(taps_ref, 0))
            + dot(lanes_ref[2], row_taps(taps_ref, 1))
        )

    later.wait()


def outer_kernel(side_ref, cross_ref, inner_ref, part_ref, taps_ref, s1, s2, s3, keep, halo_ref, lanes_ref, outer_ref):
    z, x, c = place()
    inside = jnp.where(jnp.logical_or(4 * z + 2 * x + c == 0, 4 * z + 2 * x + c == 15), 0.0, 1.0)
    halo_ref[pl.ds(pl.multiple_of(c * OWN, OWN), OWN), :] = side_ref[...]
    halo_ref[pl.ds(pl.multiple_of((1 - c) * OWN, OWN), OWN), :] = cross_ref[...]
    lay_band(halo_ref[...].astype(F32) * inside, lanes_ref)
    start = pl.multiple_of(6 * C * c, 6 * C)
    outer_ref[...] = part_ref[...] + dot(lanes_ref[...], taps_ref[pl.ds(start, 3 * C), :])
    near, far = z // 2, 1 - z // 2

    @pl.when(z % 2 == 0)
    def _():
        keep[...] = window(outer_ref, near)
        s2[...] = window(outer_ref, far)
        s1[...] = window(inner_ref, near)
        s3[...] = window(inner_ref, far)

    @pl.when(z % 2 == 1)
    def _():
        keep[...] = window(inner_ref, near)
        s2[...] = window(inner_ref, far)
        s1[...] = window(outer_ref, near)
        s3[...] = window(outer_ref, far)


def exchanged(z, step):
    low, high = z % 2, z // 2
    return (low + (step % 2) * (1 - 2 * low)) + 2 * (high + (step // 2) * (1 - 2 * high))


def add_row(step, row_ref, taps_ref, sum_ref, lanes_ref):
    z, _, _ = place()
    row = exchanged(z, step)
    act = gelu(row_ref[...])
    for tap in range(3):
        lanes_ref[:, tap * C : (tap + 1) * C] = act[8 * tap : 8 * tap + MID].astype(BF16)
    sum_ref[row + 1] += row_ref[...].astype(F32)[8 : 8 + MID]
    for tap in range(3):
        sum_ref[row + 2 - tap] += dot(lanes_ref[...], row_taps(taps_ref.at[0], tap))


def first_kernel(row_ref, taps_ref, mixed_ref, sum_ref, lanes_ref):
    sum_ref[...] = jnp.zeros_like(sum_ref)
    add_row(0, row_ref, taps_ref, sum_ref, lanes_ref)


def next_kernel(step, row_ref, taps_ref, before_ref, sum_ref, lanes_ref):
    add_row(step, row_ref, taps_ref, sum_ref, lanes_ref)


def last_kernel(step, row_ref, taps_ref, before_ref, sum_ref, parts_ref, lanes_ref, lanes3_ref, cut_ref):
    add_row(step, row_ref, taps_ref, sum_ref, lanes_ref)
    z, _, _ = place()
    half = z // 2
    for row in range(4):
        rounded = sum_ref[row + 1].astype(BF16)
        act = gelu(rounded)
        for tap in range(3):
            lanes3_ref[row, :, tap * C : (tap + 1) * C] = act[16 * tap : 16 * tap + CUT].astype(BF16)
        if row in (1, 2):
            cut_ref[row - 1] = rounded.astype(F32)[16 : 16 + CUT]
    cut_ref[0] += dot(lanes3_ref[1], row_taps(taps_ref.at[1], 1)) + dot(lanes3_ref[3], row_taps(taps_ref.at[1], 2))
    cut_ref[1] += dot(lanes3_ref[2], row_taps(taps_ref.at[1], 1)) + dot(lanes3_ref[0], row_taps(taps_ref.at[1], 0))
    for target in range(8):
        base = pl.multiple_of(8 * half + 16 * target, 8)
        left = jnp.maximum(base - 1, 0)
        right = jnp.minimum(base + 16, CUT - 1)
        for row in range(2):
            parts_ref[target, 16 * row : 16 * row + 16, :] = cut_ref[row, pl.ds(base, 16), :].astype(BF16)
        edges = [cut_ref[row, pl.ds(at, 1), :] for row in range(2) for at in (left, right)]
        parts_ref[target, 32:40, :] = jnp.concatenate(edges + edges, axis=0).astype(BF16)


def weights_kernel(taps_ref, mixed_ref):
    for tap in range(3):
        w0, w1, w2 = (taps_ref[(3 * tap + k) * C : (3 * tap + k + 1) * C, :] for k in range(3))
        ends = 0.5 * (w0.astype(F32) + w2.astype(F32))
        middle = 0.5 * w1.astype(F32)
        rows = slice(tap * C, (tap + 1) * C)
        mixed_ref[0, rows, :] = w0
        mixed_ref[1, rows, :] = (ends + middle).astype(BF16)
        mixed_ref[2, rows, :] = (ends - middle).astype(BF16)
        mixed_ref[3, rows, :] = w2


def final_kernel_body(parts_ref, mixed_ref, out_ref, ext_ref, planes_ref, lanes_ref, total_ref, done_ref, sems):
    z, x, c = place()
    target = 4 * z + 2 * x + c
    keep_first = jnp.where(target == 0, 0.0, 1.0)
    keep_last = jnp.where(target == 15, 0.0, 1.0)
    for source in range(8):
        inner, sx, sc = source // 4, (source // 2) % 2, source % 2
        rho = 4 * sx + ((0, 3), (1, 2))[inner][sc]
        edges = parts_ref[source, 32:40, :].astype(F32)
        for row in range(2):
            ext_ref[rho + 8 * row, 8:24, :] = parts_ref[source, 16 * row : 16 * row + 16, :].astype(F32)
            ext_ref[rho + 8 * row, 7:8, :] = edges[2 * row : 2 * row + 1]
            ext_ref[rho + 8 * row, 24:25, :] = edges[2 * row + 1 : 2 * row + 2]
    column = lax.broadcasted_iota(jnp.int32, (16, C), 0)
    first_mask = jnp.where(column == 0, keep_first, 1.0)
    last_mask = jnp.where(column == 15, keep_last, 1.0)
    for row in range(16):
        now = ext_ref[row, 8:24, :]
        before = ext_ref[row, 7:23, :]
        after = ext_ref[row, 9:25, :]
        u0 = (0.75 * before + 0.25 * now) * first_mask
        u1 = 0.25 * before + 0.75 * now
        u2 = 0.75 * now + 0.25 * after
        u3 = (0.25 * now + 0.75 * after) * last_mask
        planes_ref[row, 0] = u0 - u2
        planes_ref[row, 1] = u1 + u2
        planes_ref[row, 2] = u2 - u1
        planes_ref[row, 3] = u1 - u3
    zeros = jnp.zeros((16, C), BF16)
    for plane in range(4):
        lanes_ref[plane, 0:16, :] = zeros
        lanes_ref[plane, 33 * 16 : 34 * 16, :] = zeros

    def up_rows(row):
        for plane in range(4):
            value = planes_ref[row, plane]
            above, below = planes_ref[max(row - 1, 0), plane], planes_ref[min(row + 1, 15), plane]
            at = 16 * (2 * row + 1)
            lanes_ref[plane, at : at + 16, :] = (0.25 * above + 0.75 * value).astype(BF16)
            lanes_ref[plane, at + 16 : at + 32, :] = (0.75 * value + 0.25 * below).astype(BF16)

    up_rows(0)
    copies = []
    for chunk in range(32 // CHUNK):
        for row in range(CHUNK // 2 * chunk + 1, min(CHUNK // 2 * (chunk + 1) + 1, 16)):
            up_rows(row)

        def product(plane):
            return sum(
                dot(
                    lanes_ref[plane, 16 * (CHUNK * chunk + tap) : 16 * (CHUNK * (chunk + 1) + tap), :],
                    mixed_ref[plane, tap * C : (tap + 1) * C, :],
                )
                for tap in range(3)
            )

        m1 = product(1)
        m2 = product(2)
        even = m1 + m2 + product(0)
        odd = m1 - m2 - product(3)
        for lane in range(3):
            at = slice(128 * lane, 128 * lane + 128)
            total_ref[chunk, lane, pl.ds(0, 16 * CHUNK, stride=2), :] = even[:, at]
            total_ref[chunk, lane, pl.ds(1, 16 * CHUNK, stride=2), :] = odd[:, at]
        for lane in range(3):
            at = slice(128 * lane, 128 * lane + 128)
            done_ref[CHUNK * chunk : CHUNK * (chunk + 1), :, at] = (
                total_ref[chunk, lane].reshape(CHUNK, 32, 128).astype(BF16)
            )
        band = pl.ds(CHUNK * chunk, CHUNK)
        copies.append(pltpu.make_async_copy(done_ref.at[band], out_ref.at[band], sems.at[chunk]))
        copies[-1].start()
    for copy in copies:
        copy.wait()


VM = pl.BlockSpec(memory_space=pltpu.VMEM)
HBM = pl.BlockSpec(memory_space=pltpu.HBM)


def in_vmem(value):
    return pltpu.with_memory_space_constraint(value, pltpu.VMEM)


def local_call(body, operands, outs, scratch, flops, hbm_operands=(), hbm_out=False, aliases={}):
    shape = (lambda s, d: jax.ShapeDtypeStruct(s, d)) if hbm_out else pltpu.VMEM
    return pl.pallas_call(
        body,
        out_shape=tuple(shape(s, d) for s, d in outs),
        in_specs=[HBM] * len(hbm_operands) + [VM] * len(operands),
        out_specs=tuple(HBM if hbm_out else VM for _ in outs),
        scratch_shapes=scratch,
        input_output_aliases=aliases,
        compiler_params=pltpu.CompilerParams(vmem_limit_bytes=VMEM_LIMIT),
        cost_estimate=pl.CostEstimate(flops=flops, bytes_accessed=0, transcendentals=0),
    )(
        *[pltpu.with_memory_space_constraint(value, pltpu.HBM) for value in hbm_operands],
        *[in_vmem(value) for value in operands],
    )


def residue_shards(context, kernels, final_kernel):
    got = lax.ppermute(context, "gx", [(0, 1), (1, 0)])
    edge = ((OWN, C), BF16)
    cross, side = local_call(
        edge_kernel, (), [edge, edge], [pltpu.SemaphoreType.DMA((2,))], 0, hbm_operands=(context,)
    )
    chips = lax.axis_size("gy")
    places = 2 * chips
    pairs = [(0, 0), (places - 1, places - 1)]
    for left in range(1, places - 1, 2):
        pairs += [(left, left + 1), (left + 1, left)]
    cross = lax.ppermute(cross, ("gy", "gx"), pairs)
    pairs = [(places - 2, places - 1), (1, 0)]
    for chip in range(chips - 1):
        pairs += [(2 * chip, 2 * chip + 2), (2 * chip + 3, 2 * chip + 1)]
    side = lax.ppermute(side, ("gy", "gx"), pairs)

    row_flops = 2 * BAND * 3 * C * C
    win = ((WIN, C), BF16)
    row = ((BAND, C), F32)
    inner, part, taps, next_taps = local_call(
        inner_kernel,
        (got,),
        [row, row, ((9 * C, C), BF16), ((2, 9 * C, C), BF16)],
        [
            pltpu.SemaphoreType.DMA((3,)),
            pltpu.VMEM((3, OWN, C), BF16),
            pltpu.VMEM((3, BAND, C), BF16),
            pltpu.VMEM((3, BAND, 3 * C), BF16),
        ],
        5 * row_flops,
        hbm_operands=(context, kernels),
    )

    def along_z(value, step):
        pairs = [(4 * s + i, 4 * (s ^ step) + i) for s in range(4) for i in range(4)]
        return lax.ppermute(value, ("gy", "gx"), pairs)

    s1, s2, s3, keep = local_call(
        outer_kernel,
        (side, cross, inner, part, taps),
        [win] * 4,
        [pltpu.VMEM((BAND, C), BF16), pltpu.VMEM((BAND, 3 * C), BF16), pltpu.VMEM((BAND, C), F32)],
        row_flops,
    )
    sent = {3: s3, 2: s2, 1: s1}
    came = {step: along_z(sent[step], step) for step in STEPS}
    sums = ((6, MID, C), F32)
    lanes = pltpu.VMEM((MID, 3 * C), BF16)
    term_flops = 2 * MID * 9 * C * C
    (mixed,) = local_call(weights_kernel, (final_kernel,), [((4, 3 * C, C), BF16)], [], term_flops)
    (total,) = local_call(first_kernel, (keep, next_taps, mixed), [sums], [lanes], term_flops)
    for step in STEPS[:2]:
        (total,) = local_call(
            functools.partial(next_kernel, step),
            (came[step], next_taps, total),
            [sums],
            [lanes],
            term_flops,
            aliases={2: 0},
        )
    _, parts = local_call(
        functools.partial(last_kernel, STEPS[2]),
        (came[STEPS[2]], next_taps, total),
        [sums, ((8, PART, C), BF16)],
        [lanes, pltpu.VMEM((4, CUT, 3 * C), BF16), pltpu.VMEM((2, CUT, C), F32)],
        2 * term_flops,
        aliases={2: 0},
    )
    groups = [[8 * half + i for i in range(8)] for half in range(places // 8)]
    parts = lax.all_to_all(parts, ("gy", "gx"), 0, 0, axis_index_groups=groups, tiled=True)
    (out,) = local_call(
        final_kernel_body,
        (parts, mixed),
        [((32, 32, C), BF16)],
        [
            pltpu.VMEM((16, 32, C), F32),
            pltpu.VMEM((16, 4, 16, C), F32),
            pltpu.VMEM((4, 34 * 16, C), BF16),
            pltpu.VMEM((32 // CHUNK, 3, 32 * CHUNK, 128), F32),
            pltpu.VMEM((32, 32, C), BF16),
            pltpu.SemaphoreType.DMA((32 // CHUNK,)),
        ],
        2 * 512 * 12 * C * C,
        hbm_out=True,
    )
    return out


def solution(mesh):
    placed = (P(("grp", "gy"), "gx", None), P(), P())
    body = residue_shards if (mesh.shape["gy"], mesh.shape["gx"]) == (8, 2) else general_shards
    return jax.shard_map(
        body, mesh=mesh, in_specs=placed, out_specs=P("grp", ("gy", "gx"), None), check_vma=False
    )
```

```python
import functools

import jax
import jax.numpy as jnp
from jax import lax
from jax.experimental import pallas as pl
from jax.experimental.pallas import tpu as pltpu
from jax.sharding import PartitionSpec as P

dilation_list = (1, 8, 16)
F32 = jnp.float32
BF16 = jnp.bfloat16


def padded_2(cells, sides, width):
    for axis, dim in sides:
        count = lax.axis_size(axis)
        ends = count - 1
        head = lax.slice_in_dim(cells, 0, width, axis=dim)
        tail = lax.slice_in_dim(cells, cells.shape[dim] - width, cells.shape[dim], axis=dim)
        cells = jnp.concatenate(
            [
                lax.ppermute(tail, axis, [(i, (i + 1) % count) for i in range(ends)]),
                cells,
                lax.ppermute(head, axis, [((i + 1) % count, i) for i in range(ends)]),
            ],
            axis=dim,
        )
    return cells


def shifted(value, axis, by):
    size = lax.axis_size(axis)
    pairs = [(i, i + by) for i in range(size) if 0 <= i + by < size]
    return lax.ppermute(value, axis, pairs)


def activate(stream):
    return jax.nn.gelu(stream.astype(F32)).astype(BF16)


def conv_taps(row_bands, center, dilation, out_cols, kernel):
    pieces = []
    for row_band in row_bands:
        for col_tap in range(3):
            offset = center + (col_tap - 1) * dilation
            pieces.append(row_band[:, offset : offset + out_cols])
    stacked = jnp.concatenate(pieces, axis=-1)
    result = jnp.dot(
        stacked.reshape(-1, stacked.shape[-1]), kernel, preferred_element_type=F32
    )
    return result.reshape(stacked.shape[0], out_cols, kernel.shape[1])


def tile_layer(stream, kernel, dilation):
    activated = activate(stream)
    rows_here = stream.shape[0]
    if dilation == 1:
        rimmed = padded_2(activated, (("gy", 0), ("gx", 1)), 1)
        row_bands = [rimmed[0:rows_here], rimmed[1 : rows_here + 1], rimmed[2 : rows_here + 2]]
    else:
        widened = padded_2(activated, (("gx", 1),), dilation)
        hop_count = dilation // rows_here
        upper_rows = shifted(widened, "gy", hop_count)
        lower_rows = shifted(widened, "gy", -hop_count)
        row_bands = [upper_rows, widened, lower_rows]
    branch = conv_taps(row_bands, dilation, dilation, stream.shape[1], kernel)
    return (stream.astype(F32) + branch).astype(BF16)


def recut_crop(stream):
    rows_here, cols_here, channels = stream.shape
    count_gy = lax.axis_size("gy")
    count_gx = lax.axis_size("gx")
    targets = count_gy * count_gx
    grid_cols = cols_here * count_gx
    strip_cols = grid_cols // 2 // targets
    blocks = stream.reshape(rows_here, cols_here // strip_cols, strip_cols, channels)
    spare = jnp.zeros((rows_here, targets, strip_cols, channels), BF16)
    padded = jnp.concatenate([spare, blocks, spare], axis=1)
    offset = (
        targets + grid_cols // 4 // strip_cols - lax.axis_index("gx") * (cols_here // strip_cols)
    )
    outgoing = lax.dynamic_slice_in_dim(padded, offset, targets, 1)
    target = lax.axis_index(("gy", "gx"))
    owner = (grid_cols // 4 + target * strip_cols) // cols_here
    arrived = lax.all_to_all(outgoing, ("gy", "gx"), split_axis=1, concat_axis=0, tiled=True)
    arrived = arrived.reshape(count_gy, count_gx, rows_here, strip_cols, channels)
    chosen = lax.dynamic_index_in_dim(arrived, owner, 1, keepdims=False)
    grid_rows = count_gy * rows_here
    whole_rows = chosen.reshape(grid_rows, strip_cols, channels)
    return whole_rows[grid_rows // 4 : 3 * grid_rows // 4]


def widen_cols(extended):
    values = extended.astype(F32)
    inner_count = values.shape[1] - 2
    middle = values[:, 1 : inner_count + 1]
    even_cols = 0.25 * values[:, 0:inner_count] + 0.75 * middle
    odd_cols = 0.75 * middle + 0.25 * values[:, 2 : inner_count + 2]
    return jnp.stack([even_cols, odd_cols], axis=2).reshape(
        values.shape[0], 2 * inner_count, values.shape[2]
    )


def widen_rows(values):
    above = jnp.concatenate([values[:1], values[:-1]], axis=0)
    below = jnp.concatenate([values[1:], values[-1:]], axis=0)
    even_rows = 0.25 * above + 0.75 * values
    odd_rows = 0.75 * values + 0.25 * below
    return jnp.stack([even_rows, odd_rows], axis=1).reshape(
        2 * values.shape[0], values.shape[1], values.shape[2]
    )


def general_shards(context, kernels, final_kernel):
    stream = context
    for layer_index, dilation in enumerate(dilation_list):
        stream = tile_layer(stream, kernels[layer_index], dilation)
    cropped = recut_crop(stream)
    target = lax.axis_index(("gy", "gx"))
    last_target = lax.axis_size(("gy", "gx")) - 1
    rimmed = padded_2(cropped, ((("gy", "gx"), 1),), 1)
    first_col = jnp.where(target == 0, rimmed[:, 1:2], rimmed[:, 0:1])
    final_col = jnp.where(target == last_target, rimmed[:, -2:-1], rimmed[:, -1:])
    rimmed = jnp.concatenate([first_col, rimmed[:, 1:-1], final_col], axis=1)
    upsampled = widen_rows(widen_cols(rimmed)).astype(BF16)
    up_rimmed = padded_2(upsampled, ((("gy", "gx"), 1),), 1)
    up_rows = up_rimmed.shape[0]
    padded = jnp.pad(up_rimmed, ((1, 1), (0, 0), (0, 0)))
    row_bands = [padded[0:up_rows], padded[1 : up_rows + 1], padded[2 : up_rows + 2]]
    result = conv_taps(row_bands, 1, 1, up_rimmed.shape[1] - 2, final_kernel)
    return result.astype(BF16)


C = 384
OWN = 160
BAND = 320
BAND_AT = 96
WIN = 184
MID = 168
CUT = 136
PART = 40
VMEM_LIMIT = 32 * 1024 * 1024
CHUNK = 16
STEPS = (3, 1, 2)


def gelu(values):
    return jax.nn.gelu(values.astype(F32))


def dot(left, right):
    return jnp.dot(left, right, preferred_element_type=F32)


def place():
    gy = lax.axis_index("gy")
    return gy // 2, gy % 2, lax.axis_index("gx")


def row_taps(taps_ref, tap):
    return taps_ref[tap * 3 * C : (tap + 1) * 3 * C, :]


def lay_band(values, lanes_ref):
    act = gelu(values)
    lanes_ref[:, C : 2 * C] = act.astype(BF16)
    lanes_ref[:, 0:C] = pltpu.roll(act, 1, 0).astype(BF16)
    lanes_ref[:, 2 * C : 3 * C] = pltpu.roll(act, BAND - 1, 0).astype(BF16)


def window(stream_ref, half):
    start = pl.multiple_of(8 + 120 * half, 8)
    return stream_ref[pl.ds(start, WIN), :].astype(BF16)


def edge_kernel(context_ref, top_ref, low_ref, sems):
    _, _, c = place()
    at = pl.multiple_of(BAND_AT * (1 - c), 32)
    copies = [
        pltpu.make_async_copy(context_ref.at[row, pl.ds(at, OWN)], edge_ref, sems.at[slot])
        for slot, (row, edge_ref) in enumerate(((3 * c, top_ref), (3 - 3 * c, low_ref)))
    ]
    for copy in copies:
        copy.start()
    for copy in copies:
        copy.wait()


def inner_kernel(context_ref, kernels_ref, got_ref, inner_ref, part_ref, taps_ref, next_ref, sems, own_ref, band_ref, lanes_ref):
    _, _, c = place()
    at = pl.multiple_of(BAND_AT * (1 - c), 32)
    own = pltpu.make_async_copy(context_ref.at[pl.ds(c, 3), pl.ds(at, OWN)], own_ref, sems.at[0])
    taps = pltpu.make_async_copy(kernels_ref.at[0], taps_ref, sems.at[1])
    later = pltpu.make_async_copy(kernels_ref.at[pl.ds(1, 2)], next_ref, sems.at[2])
    for copy in (own, taps, later):
        copy.start()
    own.wait()
    got_at = pl.multiple_of(BAND_AT * c, 32)
    for row in range(3):
        band_ref[row, pl.ds(pl.multiple_of((1 - c) * OWN, OWN), OWN), :] = got_ref[row + c, pl.ds(got_at, OWN), :]
        band_ref[row, pl.ds(pl.multiple_of(c * OWN, OWN), OWN), :] = own_ref[row]
    for row in range(3):
        lay_band(band_ref[row], lanes_ref.at[row])
    taps.wait()
    inner_ref[...] = (
        band_ref[1].astype(F32)
        + dot(lanes_ref[0], row_taps(taps_ref, 0))
        + dot(lanes_ref[1], row_taps(taps_ref, 1))
        + dot(lanes_ref[2], row_taps(taps_ref, 2))
    )

    def taps_at(tap):
        return taps_ref[pl.ds(pl.multiple_of(3 * C * tap, 3 * C), 3 * C), :]

    part_ref[...] = (
        band_ref[2 * c].astype(F32)
        + dot(lanes_ref[c], taps_at(1 - c))
        + dot(lanes_ref[c + 1], taps_at(2 - c))
    )
    later.wait()


def outer_kernel(side_ref, cross_ref, inner_ref, part_ref, taps_ref, s1, s2, s3, keep, halo_ref, lanes_ref, outer_ref):
    z, x, c = place()
    inside = jnp.where(jnp.logical_or(4 * z + 2 * x + c == 0, 4 * z + 2 * x + c == 15), 0.0, 1.0)
    halo_ref[pl.ds(pl.multiple_of(c * OWN, OWN), OWN), :] = side_ref[...]
    halo_ref[pl.ds(pl.multiple_of((1 - c) * OWN, OWN), OWN), :] = cross_ref[...]
    lay_band(halo_ref[...].astype(F32) * inside, lanes_ref)
    start = pl.multiple_of(6 * C * c, 6 * C)
    outer_ref[...] = part_ref[...] + dot(lanes_ref[...], taps_ref[pl.ds(start, 3 * C), :])
    near, far = z // 2, 1 - z // 2

    @pl.when(z % 2 == 0)
    def _():
        keep[...] = window(outer_ref, near)
        s2[...] = window(outer_ref, far)
        s1[...] = window(inner_ref, near)
        s3[...] = window(inner_ref, far)

    @pl.when(z % 2 == 1)
    def _():
        keep[...] = window(inner_ref, near)
        s2[...] = window(inner_ref, far)
        s1[...] = window(outer_ref, near)
        s3[...] = window(outer_ref, far)


def exchanged(z, step):
    low, high = z % 2, z // 2
    return (low + (step % 2) * (1 - 2 * low)) + 2 * (high + (step // 2) * (1 - 2 * high))


def add_row(step, row_ref, taps_ref, sum_ref, lanes_ref):
    z, _, _ = place()
    row = exchanged(z, step)
    act = gelu(row_ref[...])
    for tap in range(3):
        lanes_ref[:, tap * C : (tap + 1) * C] = act[8 * tap : 8 * tap + MID].astype(BF16)
    sum_ref[row + 1] += row_ref[...].astype(F32)[8 : 8 + MID]
    for tap in range(3):
        sum_ref[row + 2 - tap] += dot(lanes_ref[...], row_taps(taps_ref.at[0], tap))


def first_kernel(row_ref, taps_ref, mixed_ref, sum_ref, lanes_ref):
    sum_ref[...] = jnp.zeros_like(sum_ref)
    add_row(0, row_ref, taps_ref, sum_ref, lanes_ref)


def next_kernel(step, row_ref, taps_ref, before_ref, sum_ref, lanes_ref):
    add_row(step, row_ref, taps_ref, sum_ref, lanes_ref)


def last_kernel(step, row_ref, taps_ref, before_ref, sum_ref, parts_ref, lanes_ref, lanes3_ref, cut_ref):
    add_row(step, row_ref, taps_ref, sum_ref, lanes_ref)
    z, _, _ = place()
    half = z // 2
    for row in range(4):
        rounded = sum_ref[row + 1].astype(BF16)
        act = gelu(rounded)
        for tap in range(3):
            lanes3_ref[row, :, tap * C : (tap + 1) * C] = act[16 * tap : 16 * tap + CUT].astype(BF16)
        if row in (1, 2):
            cut_ref[row - 1] = rounded.astype(F32)[16 : 16 + CUT]
    cut_ref[0] += dot(lanes3_ref[1], row_taps(taps_ref.at[1], 1)) + dot(lanes3_ref[3], row_taps(taps_ref.at[1], 2))
    cut_ref[1] += dot(lanes3_ref[2], row_taps(taps_ref.at[1], 1)) + dot(lanes3_ref[0], row_taps(taps_ref.at[1], 0))
    for target in range(8):
        base = pl.multiple_of(8 * half + 16 * target, 8)
        left = jnp.maximum(base - 1, 0)
        right = jnp.minimum(base + 16, CUT - 1)
        for row in range(2):
            parts_ref[target, 16 * row : 16 * row + 16, :] = cut_ref[row, pl.ds(base, 16), :].astype(BF16)
        edges = [cut_ref[row, pl.ds(at, 1), :] for row in range(2) for at in (left, right)]
        parts_ref[target, 32:40, :] = jnp.concatenate(edges + edges, axis=0).astype(BF16)


def weights_kernel(taps_ref, mixed_ref):
    for tap in range(3):
        w0, w1, w2 = (taps_ref[(3 * tap + k) * C : (3 * tap + k + 1) * C, :] for k in range(3))
        ends = 0.5 * (w0.astype(F32) + w2.astype(F32))
        middle = 0.5 * w1.astype(F32)
        rows = slice(tap * C, (tap + 1) * C)
        mixed_ref[0, rows, :] = w0
        mixed_ref[1, rows, :] = (ends + middle).astype(BF16)
        mixed_ref[2, rows, :] = (ends - middle).astype(BF16)
        mixed_ref[3, rows, :] = w2


def final_kernel_body(parts_ref, mixed_ref, out_ref, ext_ref, planes_ref, lanes_ref, total_ref, done_ref, sems):
    z, x, c = place()
    target = 4 * z + 2 * x + c
    keep_first = jnp.where(target == 0, 0.0, 1.0)
    keep_last = jnp.where(target == 15, 0.0, 1.0)
    for source in range(8):
        inner, sx, sc = source // 4, (source // 2) % 2, source % 2
        rho = 4 * sx + ((0, 3), (1, 2))[inner][sc]
        edges = parts_ref[source, 32:40, :].astype(F32)
        for row in range(2):
            ext_ref[rho + 8 * row, 8:24, :] = parts_ref[source, 16 * row : 16 * row + 16, :].astype(F32)
            ext_ref[rho + 8 * row, 7:8, :] = edges[2 * row : 2 * row + 1]
            ext_ref[rho + 8 * row, 24:25, :] = edges[2 * row + 1 : 2 * row + 2]
    column = lax.broadcasted_iota(jnp.int32, (16, C), 0)
    first_mask = jnp.where(column == 0, keep_first, 1.0)
    last_mask = jnp.where(column == 15, keep_last, 1.0)
    for row in range(16):
        now = ext_ref[row, 8:24, :]
        before = ext_ref[row, 7:23, :]
        after = ext_ref[row, 9:25, :]
        u0 = (0.75 * before + 0.25 * now) * first_mask
        u1 = 0.25 * before + 0.75 * now
        u2 = 0.75 * now + 0.25 * after
        u3 = (0.25 * now + 0.75 * after) * last_mask
        planes_ref[row, 0] = u0 - u2
        planes_ref[row, 1] = u1 + u2
        planes_ref[row, 2] = u2 - u1
        planes_ref[row, 3] = u1 - u3
    zeros = jnp.zeros((16, C), BF16)
    for plane in range(4):
        lanes_ref[plane, 0:16, :] = zeros
        lanes_ref[plane, 33 * 16 : 34 * 16, :] = zeros

    def up_rows(row):
        for plane in range(4):
            value = planes_ref[row, plane]
            above, below = planes_ref[max(row - 1, 0), plane], planes_ref[min(row + 1, 15), plane]
            at = 16 * (2 * row + 1)
            lanes_ref[plane, at : at + 16, :] = (0.25 * above + 0.75 * value).astype(BF16)
            lanes_ref[plane, at + 16 : at + 32, :] = (0.75 * value + 0.25 * below).astype(BF16)

    up_rows(0)
    copies = []
    for chunk in range(32 // CHUNK):
        for row in range(CHUNK // 2 * chunk + 1, min(CHUNK // 2 * (chunk + 1) + 1, 16)):
            up_rows(row)

        def product(plane):
            return sum(
                dot(
                    lanes_ref[plane, 16 * (CHUNK * chunk + tap) : 16 * (CHUNK * (chunk + 1) + tap), :],
                    mixed_ref[plane, tap * C : (tap + 1) * C, :],
                )
                for tap in range(3)
            )

        m1 = product(1)
        m2 = product(2)
        even = m1 + m2 + product(0)
        odd = m1 - m2 - product(3)
        for lane in range(3):
            at = slice(128 * lane, 128 * lane + 128)
            total_ref[chunk, lane, pl.ds(0, 16 * CHUNK, stride=2), :] = even[:, at]
            total_ref[chunk, lane, pl.ds(1, 16 * CHUNK, stride=2), :] = odd[:, at]
        for lane in range(3):
            at = slice(128 * lane, 128 * lane + 128)
            done_ref[CHUNK * chunk : CHUNK * (chunk + 1), :, at] = (
                total_ref[chunk, lane].reshape(CHUNK, 32, 128).astype(BF16)
            )
        band = pl.ds(CHUNK * chunk, CHUNK)
        copies.append(pltpu.make_async_copy(done_ref.at[band], out_ref.at[band], sems.at[chunk]))
        copies[-1].start()
    for copy in copies:
        copy.wait()


VM = pl.BlockSpec(memory_space=pltpu.VMEM)
HBM = pl.BlockSpec(memory_space=pltpu.HBM)


def in_vmem(value):
    return pltpu.with_memory_space_constraint(value, pltpu.VMEM)


def local_call(body, operands, outs, scratch, flops, hbm_operands=(), hbm_out=False, aliases={}):
    shape = (lambda s, d: jax.ShapeDtypeStruct(s, d)) if hbm_out else pltpu.VMEM
    return pl.pallas_call(
        body,
        out_shape=tuple(shape(s, d) for s, d in outs),
        in_specs=[HBM] * len(hbm_operands) + [VM] * len(operands),
        out_specs=tuple(HBM if hbm_out else VM for _ in outs),
        scratch_shapes=scratch,
        input_output_aliases=aliases,
        compiler_params=pltpu.CompilerParams(vmem_limit_bytes=VMEM_LIMIT),
        cost_estimate=pl.CostEstimate(flops=flops, bytes_accessed=0, transcendentals=0),
    )(
        *[pltpu.with_memory_space_constraint(value, pltpu.HBM) for value in hbm_operands],
        *[in_vmem(value) for value in operands],
    )


def residue_shards(context, kernels, final_kernel):
    got = lax.ppermute(context, "gx", [(0, 1), (1, 0)])
    edge = ((OWN, C), BF16)
    cross, side = local_call(
        edge_kernel, (), [edge, edge], [pltpu.SemaphoreType.DMA((2,))], 0, hbm_operands=(context,)
    )
    chips = lax.axis_size("gy")
    places = 2 * chips
    pairs = [(0, 0), (places - 1, places - 1)]
    for left in range(1, places - 1, 2):
        pairs += [(left, left + 1), (left + 1, left)]
    cross = lax.ppermute(cross, ("gy", "gx"), pairs)
    pairs = [(places - 2, places - 1), (1, 0)]
    for chip in range(chips - 1):
        pairs += [(2 * chip, 2 * chip + 2), (2 * chip + 3, 2 * chip + 1)]
    side = lax.ppermute(side, ("gy", "gx"), pairs)

    row_flops = 2 * BAND * 3 * C * C
    win = ((WIN, C), BF16)
    row = ((BAND, C), F32)
    inner, part, taps, next_taps = local_call(
        inner_kernel,
        (got,),
        [row, row, ((9 * C, C), BF16), ((2, 9 * C, C), BF16)],
        [
            pltpu.SemaphoreType.DMA((3,)),
            pltpu.VMEM((3, OWN, C), BF16),
            pltpu.VMEM((3, BAND, C), BF16),
            pltpu.VMEM((3, BAND, 3 * C), BF16),
        ],
        5 * row_flops,
        hbm_operands=(context, kernels),
    )

    def along_z(value, step):
        pairs = [(4 * s + i, 4 * (s ^ step) + i) for s in range(4) for i in range(4)]
        return lax.ppermute(value, ("gy", "gx"), pairs)

    s1, s2, s3, keep = local_call(
        outer_kernel,
        (side, cross, inner, part, taps),
        [win] * 4,
        [pltpu.VMEM((BAND, C), BF16), pltpu.VMEM((BAND, 3 * C), BF16), pltpu.VMEM((BAND, C), F32)],
        row_flops,
    )
    sent = {3: s3, 2: s2, 1: s1}
    came = {step: along_z(sent[step], step) for step in STEPS}
    sums = ((6, MID, C), F32)
    lanes = pltpu.VMEM((MID, 3 * C), BF16)
    term_flops = 2 * MID * 9 * C * C
    (mixed,) = local_call(weights_kernel, (final_kernel,), [((4, 3 * C, C), BF16)], [], term_flops)
    (total,) = local_call(first_kernel, (keep, next_taps, mixed), [sums], [lanes], term_flops)
    for step in STEPS[:2]:
        (total,) = local_call(
            functools.partial(next_kernel, step),
            (came[step], next_taps, total),
            [sums],
            [lanes],
            term_flops,
            aliases={2: 0},
        )
    _, parts = local_call(
        functools.partial(last_kernel, STEPS[2]),
        (came[STEPS[2]], next_taps, total),
        [sums, ((8, PART, C), BF16)],
        [lanes, pltpu.VMEM((4, CUT, 3 * C), BF16), pltpu.VMEM((2, CUT, C), F32)],
        2 * term_flops,
        aliases={2: 0},
    )
    groups = [[8 * half + i for i in range(8)] for half in range(places // 8)]
    parts = lax.all_to_all(parts, ("gy", "gx"), 0, 0, axis_index_groups=groups, tiled=True)
    (out,) = local_call(
        final_kernel_body,
        (parts, mixed),
        [((32, 32, C), BF16)],
        [
            pltpu.VMEM((16, 32, C), F32),
            pltpu.VMEM((16, 4, 16, C), F32),
            pltpu.VMEM((4, 34 * 16, C), BF16),
            pltpu.VMEM((32 // CHUNK, 3, 32 * CHUNK, 128), F32),
            pltpu.VMEM((32, 32, C), BF16),
            pltpu.SemaphoreType.DMA((32 // CHUNK,)),
        ],
        2 * 512 * 12 * C * C,
        hbm_out=True,
    )
    return out


def solution(mesh):
    placed = (P(("grp", "gy"), "gx", None), P(), P())
    body = residue_shards if (mesh.shape["gy"], mesh.shape["gx"]) == (8, 2) else general_shards
    return jax.shard_map(
        body, mesh=mesh, in_specs=placed, out_specs=P("grp", ("gy", "gx"), None), check_vma=False
    )
```

```python
import functools

import jax
import jax.numpy as jnp
from jax import lax
from jax.experimental import pallas as pl
from jax.experimental.pallas import tpu as pltpu
from jax.sharding import PartitionSpec as P

dilation_list = (1, 8, 16)
F32 = jnp.float32
BF16 = jnp.bfloat16


def padded_2(cells, sides, width):
    for axis, dim in sides:
        count = lax.axis_size(axis)
        ends = count - 1
        head = lax.slice_in_dim(cells, 0, width, axis=dim)
        tail = lax.slice_in_dim(cells, cells.shape[dim] - width, cells.shape[dim], axis=dim)
        cells = jnp.concatenate(
            [
                lax.ppermute(tail, axis, [(i, (i + 1) % count) for i in range(ends)]),
                cells,
                lax.ppermute(head, axis, [((i + 1) % count, i) for i in range(ends)]),
            ],
            axis=dim,
        )
    return cells


def shifted(value, axis, by):
    size = lax.axis_size(axis)
    pairs = [(i, i + by) for i in range(size) if 0 <= i + by < size]
    return lax.ppermute(value, axis, pairs)


def activate(stream):
    return jax.nn.gelu(stream.astype(F32)).astype(BF16)


def conv_taps(row_bands, center, dilation, out_cols, kernel):
    pieces = []
    for row_band in row_bands:
        for col_tap in range(3):
            offset = center + (col_tap - 1) * dilation
            pieces.append(row_band[:, offset : offset + out_cols])
    stacked = jnp.concatenate(pieces, axis=-1)
    result = jnp.dot(
        stacked.reshape(-1, stacked.shape[-1]), kernel, preferred_element_type=F32
    )
    return result.reshape(stacked.shape[0], out_cols, kernel.shape[1])


def tile_layer(stream, kernel, dilation):
    activated = activate(stream)
    rows_here = stream.shape[0]
    if dilation == 1:
        rimmed = padded_2(activated, (("gy", 0), ("gx", 1)), 1)
        row_bands = [rimmed[0:rows_here], rimmed[1 : rows_here + 1], rimmed[2 : rows_here + 2]]
    else:
        widened = padded_2(activated, (("gx", 1),), dilation)
        hop_count = dilation // rows_here
        upper_rows = shifted(widened, "gy", hop_count)
        lower_rows = shifted(widened, "gy", -hop_count)
        row_bands = [upper_rows, widened, lower_rows]
    branch = conv_taps(row_bands, dilation, dilation, stream.shape[1], kernel)
    return (stream.astype(F32) + branch).astype(BF16)


def recut_crop(stream):
    rows_here, cols_here, channels = stream.shape
    count_gy = lax.axis_size("gy")
    count_gx = lax.axis_size("gx")
    targets = count_gy * count_gx
    grid_cols = cols_here * count_gx
    strip_cols = grid_cols // 2 // targets
    blocks = stream.reshape(rows_here, cols_here // strip_cols, strip_cols, channels)
    spare = jnp.zeros((rows_here, targets, strip_cols, channels), BF16)
    padded = jnp.concatenate([spare, blocks, spare], axis=1)
    offset = (
        targets + grid_cols // 4 // strip_cols - lax.axis_index("gx") * (cols_here // strip_cols)
    )
    outgoing = lax.dynamic_slice_in_dim(padded, offset, targets, 1)
    target = lax.axis_index(("gy", "gx"))
    owner = (grid_cols // 4 + target * strip_cols) // cols_here
    arrived = lax.all_to_all(outgoing, ("gy", "gx"), split_axis=1, concat_axis=0, tiled=True)
    arrived = arrived.reshape(count_gy, count_gx, rows_here, strip_cols, channels)
    chosen = lax.dynamic_index_in_dim(arrived, owner, 1, keepdims=False)
    grid_rows = count_gy * rows_here
    whole_rows = chosen.reshape(grid_rows, strip_cols, channels)
    return whole_rows[grid_rows // 4 : 3 * grid_rows // 4]


def widen_cols(extended):
    values = extended.astype(F32)
    inner_count = values.shape[1] - 2
    middle = values[:, 1 : inner_count + 1]
    even_cols = 0.25 * values[:, 0:inner_count] + 0.75 * middle
    odd_cols = 0.75 * middle + 0.25 * values[:, 2 : inner_count + 2]
    return jnp.stack([even_cols, odd_cols], axis=2).reshape(
        values.shape[0], 2 * inner_count, values.shape[2]
    )


def widen_rows(values):
    above = jnp.concatenate([values[:1], values[:-1]], axis=0)
    below = jnp.concatenate([values[1:], values[-1:]], axis=0)
    even_rows = 0.25 * above + 0.75 * values
    odd_rows = 0.75 * values + 0.25 * below
    return jnp.stack([even_rows, odd_rows], axis=1).reshape(
        2 * values.shape[0], values.shape[1], values.shape[2]
    )


def general_shards(context, kernels, final_kernel):
    stream = context
    for layer_index, dilation in enumerate(dilation_list):
        stream = tile_layer(stream, kernels[layer_index], dilation)
    cropped = recut_crop(stream)
    target = lax.axis_index(("gy", "gx"))
    last_target = lax.axis_size(("gy", "gx")) - 1
    rimmed = padded_2(cropped, ((("gy", "gx"), 1),), 1)
    first_col = jnp.where(target == 0, rimmed[:, 1:2], rimmed[:, 0:1])
    final_col = jnp.where(target == last_target, rimmed[:, -2:-1], rimmed[:, -1:])
    rimmed = jnp.concatenate([first_col, rimmed[:, 1:-1], final_col], axis=1)
    upsampled = widen_rows(widen_cols(rimmed)).astype(BF16)
    up_rimmed = padded_2(upsampled, ((("gy", "gx"), 1),), 1)
    up_rows = up_rimmed.shape[0]
    padded = jnp.pad(up_rimmed, ((1, 1), (0, 0), (0, 0)))
    row_bands = [padded[0:up_rows], padded[1 : up_rows + 1], padded[2 : up_rows + 2]]
    result = conv_taps(row_bands, 1, 1, up_rimmed.shape[1] - 2, final_kernel)
    return result.astype(BF16)


C = 384
OWN = 160
BAND = 320
BAND_AT = 96
WIN = 184
MID = 168
CUT = 136
PART = 40
VMEM_LIMIT = 32 * 1024 * 1024
CHUNK = 16
STEPS = (3, 1, 2)


def gelu(values):
    return jax.nn.gelu(values.astype(F32))


def dot(left, right):
    return jnp.dot(left, right, preferred_element_type=F32)


def place():
    gy = lax.axis_index("gy")
    return gy // 2, gy % 2, lax.axis_index("gx")


def row_taps(taps_ref, tap):
    return taps_ref[tap * 3 * C : (tap + 1) * 3 * C, :]


def lay_band(values, lanes_ref):
    act = gelu(values)
    lanes_ref[:, C : 2 * C] = act.astype(BF16)
    lanes_ref[:, 0:C] = pltpu.roll(act, 1, 0).astype(BF16)
    lanes_ref[:, 2 * C : 3 * C] = pltpu.roll(act, BAND - 1, 0).astype(BF16)


def window(stream_ref, half):
    start = pl.multiple_of(8 + 120 * half, 8)
    return stream_ref[pl.ds(start, WIN), :].astype(BF16)


def edge_kernel(context_ref, top_ref, low_ref, sems):
    _, _, c = place()
    at = pl.multiple_of(BAND_AT * (1 - c), 32)
    copies = [
        pltpu.make_async_copy(context_ref.at[row, pl.ds(at, OWN)], edge_ref, sems.at[slot])
        for slot, (row, edge_ref) in enumerate(((3 * c, top_ref), (3 - 3 * c, low_ref)))
    ]
    for copy in copies:
        copy.start()
    for copy in copies:
        copy.wait()


def inner_kernel(context_ref, kernels_ref, got_ref, inner_ref, part_ref, taps_ref, sems, own_ref, band_ref, lanes_ref):
    _, _, c = place()
    at = pl.multiple_of(BAND_AT * (1 - c), 32)
    own = pltpu.make_async_copy(context_ref.at[pl.ds(c, 3), pl.ds(at, OWN)], own_ref, sems.at[0])
    taps = pltpu.make_async_copy(kernels_ref.at[0], taps_ref, sems.at[1])
    for copy in (own, taps):
        copy.start()
    own.wait()
    got_at = pl.multiple_of(BAND_AT * c, 32)
    for row in range(3):
        band_ref[row, pl.ds(pl.multiple_of((1 - c) * OWN, OWN), OWN), :] = got_ref[row + c, pl.ds(got_at, OWN), :]
        band_ref[row, pl.ds(pl.multiple_of(c * OWN, OWN), OWN), :] = own_ref[row]
    for row in range(3):
        lay_band(band_ref[row], lanes_ref.at[row])
    taps.wait()
    inner_ref[...] = (
        band_ref[1].astype(F32)
        + dot(lanes_ref[0], row_taps(taps_ref, 0))
        + dot(lanes_ref[1], row_taps(taps_ref, 1))
        + dot(lanes_ref[2], row_taps(taps_ref, 2))
    )

    def taps_at(tap):
        return taps_ref[pl.ds(pl.multiple_of(3 * C * tap, 3 * C), 3 * C), :]

    part_ref[...] = (
        band_ref[2 * c].astype(F32)
        + dot(lanes_ref[c], taps_at(1 - c))
        + dot(lanes_ref[c + 1], taps_at(2 - c))
    )


def outer_kernel(cross_ref, side_ref, inner_ref, part_ref, taps_ref, s1, s2, s3, keep, halo_ref, lanes_ref, outer_ref):
    z, x, c = place()
    inside = jnp.where(jnp.logical_or(4 * z + 2 * x + c == 0, 4 * z + 2 * x + c == 15), 0.0, 1.0)
    halo_ref[pl.ds(pl.multiple_of(c * OWN, OWN), OWN), :] = side_ref[...]
    halo_ref[pl.ds(pl.multiple_of((1 - c) * OWN, OWN), OWN), :] = cross_ref[...]
    lay_band(halo_ref[...].astype(F32) * inside, lanes_ref)
    start = pl.multiple_of(6 * C * c, 6 * C)
    outer_ref[...] = part_ref[...] + dot(lanes_ref[...], taps_ref[pl.ds(start, 3 * C), :])
    near, far = z // 2, 1 - z // 2

    @pl.when(z % 2 == 0)
    def _():
        keep[...] = window(outer_ref, near)
        s2[...] = window(outer_ref, far)
        s1[...] = window(inner_ref, near)
        s3[...] = window(inner_ref, far)

    @pl.when(z % 2 == 1)
    def _():
        keep[...] = window(inner_ref, near)
        s2[...] = window(inner_ref, far)
        s1[...] = window(outer_ref, near)
        s3[...] = window(outer_ref, far)


def exchanged(z, step):
    low, high = z % 2, z // 2
    return (low + (step % 2) * (1 - 2 * low)) + 2 * (high + (step // 2) * (1 - 2 * high))


def add_row(step, row_ref, taps_ref, sum_ref, lanes_ref):
    z, _, _ = place()
    row = exchanged(z, step)
    act = gelu(row_ref[...])
    for tap in range(3):
        lanes_ref[:, tap * C : (tap + 1) * C] = act[8 * tap : 8 * tap + MID].astype(BF16)
    sum_ref[row + 1] += row_ref[...].astype(F32)[8 : 8 + MID]
    for tap in range(3):
        sum_ref[row + 2 - tap] += dot(lanes_ref[...], row_taps(taps_ref.at[1], tap))


def first_kernel(row_ref, taps_ref, mixed_ref, sum_ref, lanes_ref):
    sum_ref[...] = jnp.zeros_like(sum_ref)
    add_row(0, row_ref, taps_ref, sum_ref, lanes_ref)


def next_kernel(step, row_ref, taps_ref, before_ref, sum_ref, lanes_ref):
    add_row(step, row_ref, taps_ref, sum_ref, lanes_ref)


def last_kernel(step, row_ref, taps_ref, before_ref, sum_ref, parts_ref, lanes_ref, lanes3_ref, cut_ref):
    add_row(step, row_ref, taps_ref, sum_ref, lanes_ref)
    z, _, _ = place()
    half = z // 2
    for row in range(4):
        rounded = sum_ref[row + 1].astype(BF16)
        act = gelu(rounded)
        for tap in range(3):
            lanes3_ref[row, :, tap * C : (tap + 1) * C] = act[16 * tap : 16 * tap + CUT].astype(BF16)
        if row in (1, 2):
            cut_ref[row - 1] = rounded.astype(F32)[16 : 16 + CUT]
    cut_ref[0] += dot(lanes3_ref[1], row_taps(taps_ref.at[2], 1)) + dot(lanes3_ref[3], row_taps(taps_ref.at[2], 2))
    cut_ref[1] += dot(lanes3_ref[2], row_taps(taps_ref.at[2], 1)) + dot(lanes3_ref[0], row_taps(taps_ref.at[2], 0))
    for target in range(8):
        base = pl.multiple_of(8 * half + 16 * target, 8)
        left = jnp.maximum(base - 1, 0)
        right = jnp.minimum(base + 16, CUT - 1)
        for row in range(2):
            parts_ref[target, 16 * row : 16 * row + 16, :] = cut_ref[row, pl.ds(base, 16), :].astype(BF16)
        edges = [cut_ref[row, pl.ds(at, 1), :] for row in range(2) for at in (left, right)]
        parts_ref[target, 32:40, :] = jnp.concatenate(edges + edges, axis=0).astype(BF16)


def weights_kernel(taps_ref, mixed_ref):
    for tap in range(3):
        w0, w1, w2 = (taps_ref[(3 * tap + k) * C : (3 * tap + k + 1) * C, :] for k in range(3))
        ends = 0.5 * (w0.astype(F32) + w2.astype(F32))
        middle = 0.5 * w1.astype(F32)
        rows = slice(tap * C, (tap + 1) * C)
        mixed_ref[0, rows, :] = w0
        mixed_ref[1, rows, :] = (ends + middle).astype(BF16)
        mixed_ref[2, rows, :] = (ends - middle).astype(BF16)
        mixed_ref[3, rows, :] = w2


def final_kernel_body(parts_ref, mixed_ref, out_ref, ext_ref, planes_ref, lanes_ref, total_ref, done_ref, sems):
    z, x, c = place()
    target = 4 * z + 2 * x + c
    keep_first = jnp.where(target == 0, 0.0, 1.0)
    keep_last = jnp.where(target == 15, 0.0, 1.0)
    for source in range(8):
        inner, sx, sc = source // 4, (source // 2) % 2, source % 2
        rho = 4 * sx + ((0, 3), (1, 2))[inner][sc]
        edges = parts_ref[source, 32:40, :].astype(F32)
        for row in range(2):
            ext_ref[rho + 8 * row, 8:24, :] = parts_ref[source, 16 * row : 16 * row + 16, :].astype(F32)
            ext_ref[rho + 8 * row, 7:8, :] = edges[2 * row : 2 * row + 1]
            ext_ref[rho + 8 * row, 24:25, :] = edges[2 * row + 1 : 2 * row + 2]
    column = lax.broadcasted_iota(jnp.int32, (16, C), 0)
    first_mask = jnp.where(column == 0, keep_first, 1.0)
    last_mask = jnp.where(column == 15, keep_last, 1.0)
    for row in range(16):
        now = ext_ref[row, 8:24, :]
        before = ext_ref[row, 7:23, :]
        after = ext_ref[row, 9:25, :]
        u0 = (0.75 * before + 0.25 * now) * first_mask
        u1 = 0.25 * before + 0.75 * now
        u2 = 0.75 * now + 0.25 * after
        u3 = (0.25 * now + 0.75 * after) * last_mask
        planes_ref[row, 0] = u0 - u2
        planes_ref[row, 1] = u1 + u2
        planes_ref[row, 2] = u2 - u1
        planes_ref[row, 3] = u1 - u3
    zeros = jnp.zeros((16, C), BF16)
    for plane in range(4):
        lanes_ref[plane, 0:16, :] = zeros
        lanes_ref[plane, 33 * 16 : 34 * 16, :] = zeros

    def up_rows(row):
        for plane in range(4):
            value = planes_ref[row, plane]
            above, below = planes_ref[max(row - 1, 0), plane], planes_ref[min(row + 1, 15), plane]
            at = 16 * (2 * row + 1)
            lanes_ref[plane, at : at + 16, :] = (0.25 * above + 0.75 * value).astype(BF16)
            lanes_ref[plane, at + 16 : at + 32, :] = (0.75 * value + 0.25 * below).astype(BF16)

    up_rows(0)
    copies = []
    for chunk in range(32 // CHUNK):
        for row in range(CHUNK // 2 * chunk + 1, min(CHUNK // 2 * (chunk + 1) + 1, 16)):
            up_rows(row)

        def product(plane):
            return sum(
                dot(
                    lanes_ref[plane, 16 * (CHUNK * chunk + tap) : 16 * (CHUNK * (chunk + 1) + tap), :],
                    mixed_ref[plane, tap * C : (tap + 1) * C, :],
                )
                for tap in range(3)
            )

        m1 = product(1)
        m2 = product(2)
        even = m1 + m2 + product(0)
        odd = m1 - m2 - product(3)
        for lane in range(3):
            at = slice(128 * lane, 128 * lane + 128)
            total_ref[chunk, lane, pl.ds(0, 16 * CHUNK, stride=2), :] = even[:, at]
            total_ref[chunk, lane, pl.ds(1, 16 * CHUNK, stride=2), :] = odd[:, at]
        for lane in range(3):
            at = slice(128 * lane, 128 * lane + 128)
            done_ref[CHUNK * chunk : CHUNK * (chunk + 1), :, at] = (
                total_ref[chunk, lane].reshape(CHUNK, 32, 128).astype(BF16)
            )
        band = pl.ds(CHUNK * chunk, CHUNK)
        copies.append(pltpu.make_async_copy(done_ref.at[band], out_ref.at[band], sems.at[chunk]))
        copies[-1].start()
    for copy in copies:
        copy.wait()


VM = pl.BlockSpec(memory_space=pltpu.VMEM)
HBM = pl.BlockSpec(memory_space=pltpu.HBM)


def in_vmem(value):
    return pltpu.with_memory_space_constraint(value, pltpu.VMEM)


def local_call(body, operands, outs, scratch, flops, hbm_operands=(), hbm_out=False, aliases={}):
    shape = (lambda s, d: jax.ShapeDtypeStruct(s, d)) if hbm_out else pltpu.VMEM
    return pl.pallas_call(
        body,
        out_shape=tuple(shape(s, d) for s, d in outs),
        in_specs=[HBM] * len(hbm_operands) + [VM] * len(operands),
        out_specs=tuple(HBM if hbm_out else VM for _ in outs),
        scratch_shapes=scratch,
        input_output_aliases=aliases,
        compiler_params=pltpu.CompilerParams(vmem_limit_bytes=VMEM_LIMIT),
        cost_estimate=pl.CostEstimate(flops=flops, bytes_accessed=0, transcendentals=0),
    )(
        *[pltpu.with_memory_space_constraint(value, pltpu.HBM) for value in hbm_operands],
        *[in_vmem(value) for value in operands],
    )


def residue_shards(context, kernels, final_kernel):
    got = lax.ppermute(context, "gx", [(0, 1), (1, 0)])
    edge = ((OWN, C), BF16)
    cross, side = local_call(
        edge_kernel, (), [edge, edge], [pltpu.SemaphoreType.DMA((2,))], 0, hbm_operands=(context,)
    )
    chips = lax.axis_size("gy")
    places = 2 * chips
    pairs = [(0, 0), (places - 1, places - 1)]
    for left in range(1, places - 1, 2):
        pairs += [(left, left + 1), (left + 1, left)]
    cross = lax.ppermute(cross, ("gy", "gx"), pairs)
    pairs = [(places - 2, places - 1), (1, 0)]
    for chip in range(chips - 1):
        pairs += [(2 * chip, 2 * chip + 2), (2 * chip + 3, 2 * chip + 1)]
    side = lax.ppermute(side, ("gy", "gx"), pairs)

    row_flops = 2 * BAND * 3 * C * C
    win = ((WIN, C), BF16)
    row = ((BAND, C), F32)
    inner, part, taps = local_call(
        inner_kernel,
        (got,),
        [row, row, ((9 * C, C), BF16)],
        [
            pltpu.SemaphoreType.DMA((2,)),
            pltpu.VMEM((3, OWN, C), BF16),
            pltpu.VMEM((3, BAND, C), BF16),
            pltpu.VMEM((3, BAND, 3 * C), BF16),
        ],
        5 * row_flops,
        hbm_operands=(context, kernels),
    )

    def along_z(value, step):
        pairs = [(4 * s + i, 4 * (s ^ step) + i) for s in range(4) for i in range(4)]
        return lax.ppermute(value, ("gy", "gx"), pairs)

    s1, s2, s3, keep = local_call(
        outer_kernel,
        (cross, side, inner, part, taps),
        [win] * 4,
        [pltpu.VMEM((BAND, C), BF16), pltpu.VMEM((BAND, 3 * C), BF16), pltpu.VMEM((BAND, C), F32)],
        row_flops,
    )
    sent = {3: s3, 2: s2, 1: s1}
    came = {step: along_z(sent[step], step) for step in STEPS}
    sums = ((6, MID, C), F32)
    lanes = pltpu.VMEM((MID, 3 * C), BF16)
    term_flops = 2 * MID * 9 * C * C
    (mixed,) = local_call(weights_kernel, (final_kernel,), [((4, 3 * C, C), BF16)], [], term_flops)
    (total,) = local_call(first_kernel, (keep, kernels, mixed), [sums], [lanes], term_flops)
    for step in STEPS[:2]:
        (total,) = local_call(
            functools.partial(next_kernel, step),
            (came[step], kernels, total),
            [sums],
            [lanes],
            term_flops,
            aliases={2: 0},
        )
    _, parts = local_call(
        functools.partial(last_kernel, STEPS[2]),
        (came[STEPS[2]], kernels, total),
        [sums, ((8, PART, C), BF16)],
        [lanes, pltpu.VMEM((4, CUT, 3 * C), BF16), pltpu.VMEM((2, CUT, C), F32)],
        2 * term_flops,
        aliases={2: 0},
    )
    groups = [[8 * half + i for i in range(8)] for half in range(places // 8)]
    parts = lax.all_to_all(parts, ("gy", "gx"), 0, 0, axis_index_groups=groups, tiled=True)
    (out,) = local_call(
        final_kernel_body,
        (parts, mixed),
        [((32, 32, C), BF16)],
        [
            pltpu.VMEM((16, 32, C), F32),
            pltpu.VMEM((16, 4, 16, C), F32),
            pltpu.VMEM((4, 34 * 16, C), BF16),
            pltpu.VMEM((32 // CHUNK, 3, 32 * CHUNK, 128), F32),
            pltpu.VMEM((32, 32, C), BF16),
            pltpu.SemaphoreType.DMA((32 // CHUNK,)),
        ],
        2 * 512 * 12 * C * C,
        hbm_out=True,
    )
    return out


def solution(mesh):
    placed = (P(("grp", "gy"), "gx", None), P(), P())
    body = residue_shards if (mesh.shape["gy"], mesh.shape["gx"]) == (8, 2) else general_shards
    return jax.shard_map(
        body, mesh=mesh, in_specs=placed, out_specs=P("grp", ("gy", "gx"), None), check_vma=False
    )
```
